256 devices in a mesh: seq: 64 (over x, z, core), head: 4 (over y).
Axes of the slice: x: 4, y: 4, z: 8, core: 2. Of those that a mesh axis runs over, the one named last changes fastest.
Arguments:
- queries: bfloat16 [8192, 1024], P(('seq', 'head')), may hold values from -20 to 20
- keys: bfloat16 [8192, 1024], P(('seq', 'head')), may hold values from -8 to 8
- values: bfloat16 [8192, 1024], P(('seq', 'head')), may hold values from -6 to 6
- block_mask: int32 [8, 64, 64], P('head', 'seq'), may hold values from 0 to 1, as said below
- out_weight: bfloat16 [1024, 5120], P('head'), may hold values from -1.5 to 1.5
Outputs:
- mixed: bfloat16 [8192, 5120], P(('seq', 'head'))
The draws below stay inside these ranges and needn't reach their ends.
Inputs may be any that keep to these rules, and one draw needn't show every extreme that they name: `block_mask`: every head's diagonal blocks are 1.
All inputs are finite; a program needn't handle non-finite values.
Results may differ from the reference program's by a relative error of at most 0.015.
Values may be sent and summed in bfloat16 or wider, within the bound.
No kernel may reach another device: no remote copies, remote signals or barrier semaphores. Data moves between devices by JAX's collectives and lax.ppermute only.
A program may use at most 64 MiB of HBM per device.

```python
import math
import jax
import jax.numpy as jnp
from jax import lax

D = 5120
HD = 128
HEADS = 8
BLK = 128
LEN = 8192
NB = 64


def key_field(key):
    normal = jnp.clip(jax.random.normal(key, (LEN, HEADS * HD), jnp.float32), -3.5, 3.5)
    field = 1.5 * normal
    rows = jnp.arange(LEN)
    first = rows % (5 * BLK) == 5
    second = rows % (5 * BLK) == 6
    scaled = field
    before = jnp.roll(scaled, 1, axis=0)
    return jnp.where(first[:, None], scaled, jnp.where(second[:, None], 0.99 * before, field))


def draw_keys(key, part):
    field = key_field(key)
    return field.astype(jnp.bfloat16)


def draw_queries(key, part):
    own = jax.random.fold_in(key, 7)
    result = 1.5 * jnp.clip(jax.random.normal(own, (LEN, HEADS * HD), jnp.float32), -3.5, 3.5)
    return result.astype(jnp.bfloat16)


def draw_block_mask(key, part):
    key = jax.random.fold_in(key, 3)
    level_key, ticket_key = jax.random.split(key)
    level = jax.random.randint(level_key, (HEADS, NB, 1), 4, 11)
    limit = jnp.left_shift(jnp.ones_like(level), level)
    ticket = jax.random.randint(ticket_key, (HEADS, NB, NB), 0, 1024)
    diagonal = jnp.arange(NB)[:, None] == jnp.arange(NB)[None, :]
    return jnp.where((ticket < limit) | diagonal[None, :, :], 1, 0).astype(jnp.int32)


def shard_levels(key, shape, cuts, low, largest):
    def one(position, blocks):
        draws = jax.random.uniform(jax.random.fold_in(jax.random.fold_in(key, 6), position), (blocks,), jnp.float32, low / len(cuts), largest / len(cuts))
        return jnp.repeat(jnp.exp(draws), shape[position] // blocks).reshape((-1,) + (1,) * (len(shape) - position - 1))

    gain = one(*cuts[0])
    for cut in cuts[1:]:
        gain = gain * one(*cut)
    return gain


def scatter_about(rng, dims, spread, reach, shards=(), held_as=jnp.bfloat16):
    values = spread * jax.random.normal(rng, dims, jnp.float32)
    if shards:
        values = values * shard_levels(rng, dims, shards, -0.22, 0.18)
    return jnp.clip(values, -reach, reach).astype(held_as)


def setup_inputs(seed: int = 0) -> dict:
    arg_keys = jax.random.split(jax.random.key(seed), 6)
    return {
        "queries": draw_queries(jax.random.fold_in(arg_keys[5], 71), 0),
        "keys": draw_keys(jax.random.fold_in(arg_keys[5], 71), 0),
        "values": scatter_about(arg_keys[2], (LEN, HEADS * HD), 1.0, 6.0, ((0, 256),)),
        "block_mask": draw_block_mask(jax.random.fold_in(arg_keys[5], 71), 0),
        "out_weight": scatter_about(arg_keys[4], (HEADS * HD, D), (HEADS * HD // 64) ** -0.5, 1.5, ((0, 4),)),
    }


def reference(queries, keys, values, block_mask, out_weight):
    scale = 1.0 / math.sqrt(HD)
    rows = min(512, LEN)
    key_block = (jnp.arange(LEN) // BLK).astype(jnp.int32)

    def head_part(head):
        start_col = (head * HD).astype(jnp.int32)
        q_head = lax.dynamic_slice_in_dim(queries, start_col, HD, 1)
        k_head = lax.dynamic_slice_in_dim(keys, start_col, HD, 1)
        v_head = lax.dynamic_slice_in_dim(values, start_col, HD, 1)
        mask_head = block_mask[head]

        def query_part(index):
            first = (index * rows).astype(jnp.int32)
            q_rows = lax.dynamic_slice_in_dim(q_head, first, rows, 0)
            scores = jnp.dot(q_rows, k_head.T, preferred_element_type=jnp.float32) * scale
            q_block = ((first + jnp.arange(rows)) // BLK).astype(jnp.int32)
            allowed = mask_head[q_block][:, key_block] > 0
            top = lax.optimization_barrier(jnp.max(jnp.where(allowed, scores, -1e+30), axis=1, keepdims=True))
            weights = jnp.where(allowed, jnp.exp(scores - top), 0.0)
            total = lax.optimization_barrier(jnp.sum(weights, axis=1, keepdims=True))
            mixed_rows = jnp.dot(weights.astype(jnp.bfloat16), v_head, preferred_element_type=jnp.float32) / total
            return mixed_rows.astype(jnp.bfloat16)
        return lax.map(query_part, jnp.arange(LEN // rows).astype(jnp.int32))
    outputs = lax.map(head_part, jnp.arange(HEADS).astype(jnp.int32))
    attn = outputs.reshape(HEADS, LEN, HD).transpose(1, 0, 2).reshape(LEN, HEADS * HD)
    return jnp.dot(attn, out_weight, preferred_element_type=jnp.float32).astype(jnp.bfloat16)
```

```python
import functools
import math

import jax
import jax.numpy as jnp
from jax import lax
from jax.experimental import pallas as pl
from jax.experimental.pallas import tpu as pltpu
from jax.sharding import Mesh, PartitionSpec as P

HD = 128
BLK = 128
NX, NH, NL, NC, NY = 4, 4, 2, 2, 4
AXES = ("x", "zh", "zl", "c", "y")
SIZES = (NX, NH, NL, NC, NY)
BF = jnp.bfloat16
F32 = jnp.float32
SCALE2 = math.log2(math.e) / math.sqrt(HD)
NEG = -1e30
BIG = 1e30
VMEM = pl.BlockSpec(memory_space=pltpu.VMEM)
SMEM = pl.BlockSpec(memory_space=pltpu.SMEM)
PARAMS = pltpu.CompilerParams(vmem_limit_bytes=40 * 2**20)


def moved(value, axis, by):
    size = SIZES[AXES.index(axis)]
    return lax.ppermute(value, axis, [(i, (i + by) % size) for i in range(size)])


def prep_kernel(q_ref, k_ref, v_ref, out_ref):
    for c in range(NC):
        for y in range(NY):
            cols = pl.ds((2 * y + c) * HD, HD)
            for i, ref in enumerate((q_ref, k_ref, v_ref)):
                out_ref[c * NY + y, :, i * HD : (i + 1) * HD] = ref[:, cols]


def mid_kernel(where_ref, got_ref, own_ref, other_ref, q_ref, kv_ref):
    y, c = where_ref[4], where_ref[3]
    for part in range(NC):
        for p in range(NY):
            rows = pl.ds((part * NY + p) * 32, 32)
            q_ref[rows, :] = got_ref[part * NY + lax.rem(y + p, NY), :, :HD]
            kv_ref[rows, :] = got_ref[part * NY + p, :, HD:]
    own, other = own_ref[...].astype(F32), other_ref[...].astype(F32)
    first = lax.broadcasted_iota(jnp.int32, own.shape, 0) < 8
    q_ref[256:, :] = jnp.where(first == (c == 0), own, other).astype(BF)


def attend_kernel(where_ref, mask_ref, *refs):
    q_refs, kv_refs, out_refs = refs[:4], refs[4:12], refs[12:16]
    vt_ref, s_ref, p_ref = refs[16:]
    x, zh, zl = where_ref[0], where_ref[1], where_ref[2]
    for i in range(8):
        vt_ref[:, i * 256 : (i + 1) * 256] = kv_refs[i][:, HD:].T
    first = lax.broadcasted_iota(jnp.int32, (1, 256), 1) < BLK
    for j in range(4):
        q = q_refs[j][:256, :]
        opens = []
        top = jnp.full((1, 256), NEG, F32)
        for i in range(8):
            step, flip = i % 4, i // 4
            source = lax.rem(x + NX - step, NX) * 16 + zh * 4 + lax.rem(zl + flip, 2) * 2
            s = lax.dot_general(
                kv_refs[i][:, :HD], q, (((1,), (1,)), ((), ())), preferred_element_type=F32
            )
            s_ref[i * 256 : (i + 1) * 256, :] = s
            for part in range(2):
                open0 = mask_ref[2 * j, source + part]
                open1 = mask_ref[2 * j + 1, source + part]
                is_open = jnp.where(first, open0, open1) > 0
                opens.append(is_open)
                here = jnp.max(s[part * BLK : (part + 1) * BLK], axis=0, keepdims=True)
                top = jnp.maximum(top, jnp.where(is_open, here, NEG))
        top = top * SCALE2
        total = jnp.zeros((1, 256), F32)
        for b in range(16):
            less = jnp.where(opens[b], top, BIG)
            rows = slice(b * BLK, (b + 1) * BLK)
            w = jnp.exp2(s_ref[rows, :] * SCALE2 - less)
            total += jnp.sum(w, axis=0, keepdims=True)
            p_ref[rows, :] = w.astype(BF)
        acc = jnp.dot(vt_ref[...], p_ref[...], preferred_element_type=F32)
        some = total > 0.0
        safe = jnp.where(some, total, 1.0)
        out_refs[j][:HD, :] = (acc / safe).astype(BF)
        lse = jnp.where(some, top + jnp.log2(safe), NEG)
        hi = lse.astype(BF).astype(F32)
        mid = (lse - hi).astype(BF).astype(F32)
        low = lse - hi - mid
        row = lax.broadcasted_iota(jnp.int32, (16, 256), 0)
        out_refs[j][HD:, :] = jnp.where(row == 0, hi, jnp.where(row == 1, mid, low)).astype(BF)


def merge_kernel(where_ref, a_ref, b_ref, c_ref, d_ref, keep_ref, send_ref):
    refs = (a_ref, b_ref, c_ref, d_ref)
    lses = []
    for ref in refs:
        tail = ref[HD:, :].astype(F32)
        lses.append(tail[0:1] + tail[1:2] + tail[2:3])
    top = functools.reduce(jnp.maximum, lses)
    ws = [jnp.exp2(lse - top) for lse in lses]
    inv = 1.0 / sum(ws)
    acc = sum(ref[:HD, :].astype(F32) * (w * inv) for ref, w in zip(refs, ws))
    left, right = acc[:, :BLK].astype(BF), acc[:, BLK:].astype(BF)

    @pl.when(where_ref[3] == 0)
    def _():
        keep_ref[...] = left
        send_ref[...] = right

    @pl.when(where_ref[3] == 1)
    def _():
        keep_ref[...] = right
        send_ref[...] = left


def project_kernel(where_ref, own_ref, other_ref, w_ref, *refs):
    out_refs, lhs_ref = refs[:4], refs[4]

    @pl.when(pl.program_id(0) == 0)
    def _():
        own, other = own_ref[...].T, other_ref[...].T

        @pl.when(where_ref[3] == 0)
        def _():
            lhs_ref[:, :HD] = own
            lhs_ref[:, HD:] = other

        @pl.when(where_ref[3] == 1)
        def _():
            lhs_ref[:, :HD] = other
            lhs_ref[:, HD:] = own

    out = jnp.dot(lhs_ref[...], w_ref[...], preferred_element_type=F32).astype(BF)
    for p in range(NY):
        out_refs[p][...] = out[p * 32 : (p + 1) * 32]


def sum_kernel(a_ref, b_ref, c_ref, d_ref, out_ref):
    out_ref[...] = (
        a_ref[...].astype(F32)
        + b_ref[...].astype(F32)
        + c_ref[...].astype(F32)
        + d_ref[...].astype(F32)
    ).astype(BF)


def shape(*dims, dtype=BF):
    return jax.ShapeDtypeStruct(dims, dtype)


def body(queries, keys, values, block_mask, out_weight):
    where = jnp.stack([lax.axis_index(a) for a in AXES]).astype(jnp.int32)
    core = lax.axis_index("c")
    seen = jnp.pad(block_mask[:, 0, :].astype(BF), ((0, 0), (0, 64)))
    own_mask = jnp.broadcast_to(lax.dynamic_slice_in_dim(seen, core, 1), (16, 128))
    send_mask = jnp.broadcast_to(lax.dynamic_slice_in_dim(seen, 1 - core, 1), (16, 128))
    other_mask = moved(send_mask, "c", 1)

    packed = pl.pallas_call(
        prep_kernel,
        out_shape=shape(8, 32, 384),
        in_specs=[VMEM] * 3,
        out_specs=VMEM,
        compiler_params=PARAMS,
    )(queries, keys, values)
    got = lax.all_to_all(packed, ("c", "y"), split_axis=0, concat_axis=0, tiled=True)
    q, kv = pl.pallas_call(
        mid_kernel,
        out_shape=(shape(272, HD), shape(256, 256)),
        in_specs=[SMEM] + [VMEM] * 3,
        out_specs=(VMEM, VMEM),
        compiler_params=PARAMS,
    )(where, got, own_mask, other_mask)

    pair = moved(kv, "zl", 1)
    kvs = [kv] + [moved(kv, "x", k) for k in (1, 2, 3)]
    qs = [q] + [moved(q, "zh", k) for k in (1, 2, 3)]
    kvs += [pair] + [moved(pair, "x", k) for k in (1, 2, 3)]
    mask = jnp.concatenate([t[r : r + 1, :64] for t in qs for r in (256, 264)]).astype(jnp.int32)

    parts = pl.pallas_call(
        attend_kernel,
        out_shape=tuple(shape(144, 256) for _ in range(4)),
        in_specs=[SMEM] * 2 + [VMEM] * 12,
        out_specs=(VMEM,) * 4,
        scratch_shapes=[
            pltpu.VMEM((HD, 2048), BF),
            pltpu.VMEM((2048, 256), F32),
            pltpu.VMEM((2048, 256), BF),
        ],
        compiler_params=PARAMS,
        cost_estimate=pl.CostEstimate(
            flops=2 * 2 * 1024 * 2048 * HD, bytes_accessed=2**21, transcendentals=2**21
        ),
    )(where, mask, *qs, *kvs)
    back = [parts[0]] + [moved(parts[k], "zh", -k) for k in (1, 2, 3)]

    keep, send = pl.pallas_call(
        merge_kernel,
        out_shape=(shape(HD, BLK), shape(HD, BLK)),
        in_specs=[SMEM] + [VMEM] * 4,
        out_specs=(VMEM, VMEM),
        compiler_params=PARAMS,
    )(where, *back)
    other = moved(send, "c", 1)

    cols = 1280
    width = out_weight.shape[1]
    pieces = pl.pallas_call(
        project_kernel,
        out_shape=tuple(shape(32, width) for _ in range(4)),
        grid=(width // cols,),
        in_specs=[
            SMEM,
            pl.BlockSpec((HD, BLK), lambda i: (0, 0)),
            pl.BlockSpec((HD, BLK), lambda i: (0, 0)),
            pl.BlockSpec((2 * HD, cols), lambda i: (0, i)),
        ],
        out_specs=tuple(pl.BlockSpec((32, cols), lambda i: (0, i)) for _ in range(4)),
        scratch_shapes=[pltpu.VMEM((BLK, 2 * HD), BF)],
        compiler_params=PARAMS,
        cost_estimate=pl.CostEstimate(
            flops=2 * 128 * 256 * width, bytes_accessed=2**22, transcendentals=0
        ),
    )(where, keep, other, out_weight)
    arrived = [moved(pieces[k], "y", k) for k in (2, 1, 3)]
    return pl.pallas_call(
        sum_kernel,
        out_shape=shape(32, width),
        in_specs=[VMEM] * 4,
        out_specs=VMEM,
        compiler_params=PARAMS,
    )(pieces[0], *arrived)


def solution(mesh):
    grid = Mesh(mesh.devices.reshape(SIZES), AXES)
    rows = P(AXES, None)
    in_specs = (rows, rows, rows, P("y", AXES[:4], None), P("y", None))
    return jax.shard_map(body, mesh=grid, in_specs=in_specs, out_specs=rows, check_vma=False)
```

```python
import functools
import math

import jax
import jax.numpy as jnp
from jax import lax
from jax.experimental import pallas as pl
from jax.experimental.pallas import tpu as pltpu
from jax.sharding import Mesh, PartitionSpec as P

HD = 128
BLK = 128
NX, NH, NL, NC, NY = 4, 4, 2, 2, 4
AXES = ("x", "zh", "zl", "c", "y")
SIZES = (NX, NH, NL, NC, NY)
BF = jnp.bfloat16
F32 = jnp.float32
SCALE2 = math.log2(math.e) / math.sqrt(HD)
NEG = -1e30
BIG = 1e30
VMEM = pl.BlockSpec(memory_space=pltpu.VMEM)
SMEM = pl.BlockSpec(memory_space=pltpu.SMEM)
PARAMS = pltpu.CompilerParams(vmem_limit_bytes=40 * 2**20)


def moved(value, axis, by):
    size = SIZES[AXES.index(axis)]
    return lax.ppermute(value, axis, [(i, (i + by) % size) for i in range(size)])


def moved_by_core(value, axis):
    size = SIZES[AXES.index(axis)]
    pairs = []
    for i in range(size):
        pairs.append((i * 2, (i + 1) % size * 2))
        pairs.append((i * 2 + 1, (i - 1) % size * 2 + 1))
    return lax.ppermute(value, (axis, "c"), pairs)


def prep_kernel(q_ref, k_ref, v_ref, out_ref, held_ref, sem):
    copies = [
        pltpu.make_async_copy(ref, held_ref.at[i], sem.at[i])
        for i, ref in enumerate((q_ref, k_ref, v_ref))
    ]
    for copy in copies:
        copy.start()
    for i, copy in enumerate(copies):
        copy.wait()
        for c in range(NC):
            for y in range(NY):
                cols = slice((2 * y + c) * HD, (2 * y + c + 1) * HD)
                out_ref[c * NY + y, :, i * HD : (i + 1) * HD] = held_ref[i, :, cols]


def mid_kernel(where_ref, got_ref, own_ref, other_ref, q_ref, kv_ref):
    y, c = where_ref[4], where_ref[3]
    for part in range(NC):
        for p in range(NY):
            rows = pl.ds((part * NY + p) * 32, 32)
            q_ref[rows, :] = got_ref[part * NY + lax.rem(y + p, NY), :, :HD]
            kv_ref[rows, :] = got_ref[part * NY + p, :, HD:]
    own, other = own_ref[...].astype(F32), other_ref[...].astype(F32)
    first = lax.broadcasted_iota(jnp.int32, own.shape, 0) < 8
    q_ref[256:, :] = jnp.where(first == (c == 0), own, other).astype(BF)


def attend_kernel(where_ref, *refs):
    q_refs, kv_refs = refs[:4], refs[4:12]
    own_ref, plus_ref, minus_ref, across_ref = refs[12:16]
    vt_ref, s_ref, p_ref, open_ref = refs[16:]
    x, zh, zl, core = where_ref[0], where_ref[1], where_ref[2], where_ref[3]
    for i in range(8):
        vt_ref[:, i * 256 : (i + 1) * 256] = kv_refs[i][:, HD:].T
    masks = jnp.concatenate([ref[256:272, :] for ref in q_refs], axis=0)
    row = lax.broadcasted_iota(jnp.int32, (64, 1024), 0)
    block = lax.broadcasted_iota(jnp.int32, (64, 1024), 1) // BLK
    pick = jnp.where(row == block * 8, 1.0, 0.0).astype(BF)
    open_ref[...] = lax.dot_general(
        masks, pick, (((0,), (0,)), ((), ())), preferred_element_type=F32
    )
    for j in range(4):
        q = q_refs[j][:256, :]
        slot = j % 2
        opens = []
        top = jnp.full((1, 256), NEG, F32)
        for i in range(8):
            step, flip = i % 4, i // 4
            source = lax.rem(x + NX - step, NX) * 16 + zh * 4 + lax.rem(zl + flip, 2) * 2
            s = lax.dot_general(
                kv_refs[i][:, :HD], q, (((1,), (1,)), ((), ())), preferred_element_type=F32
            )
            s_ref[slot, i * 256 : (i + 1) * 256, :] = s
            for part in range(2):
                is_open = open_ref[pl.ds(source + part, 1), j * 256 : (j + 1) * 256] > 0.5
                opens.append(is_open)
                here = jnp.max(s[part * BLK : (part + 1) * BLK], axis=0, keepdims=True)
                top = jnp.maximum(top, jnp.where(is_open, here, NEG))
        top = top * SCALE2
        total = jnp.zeros((1, 256), F32)
        for b in range(16):
            less = jnp.where(opens[b], top, BIG)
            rows = slice(b * BLK, (b + 1) * BLK)
            w = jnp.exp2(s_ref[slot, rows, :] * SCALE2 - less)
            total += jnp.sum(w, axis=0, keepdims=True)
            p_ref[slot, rows, :] = w.astype(BF)
        acc = jnp.dot(vt_ref[...], p_ref[slot], preferred_element_type=F32)
        some = total > 0.0
        safe = jnp.where(some, total, 1.0)
        out = (acc / safe).astype(BF)
        lse = jnp.where(some, top + jnp.log2(safe), NEG)
        hi = lse.astype(BF).astype(F32)
        mid = (lse - hi).astype(BF).astype(F32)
        low = lse - hi - mid
        row = lax.broadcasted_iota(jnp.int32, (16, 256), 0)
        tail = jnp.where(row == 0, hi, jnp.where(row == 1, mid, low)).astype(BF)

        def put(ref, out=out, tail=tail):
            ref[:HD, :] = out
            ref[HD:, :] = tail

        if j == 0:
            put(own_ref)
        elif j == 2:
            put(across_ref)
        else:
            pl.when(core == (j == 3))(functools.partial(put, minus_ref))
            pl.when(core != (j == 3))(functools.partial(put, plus_ref))


def merge_kernel(where_ref, a_ref, b_ref, c_ref, d_ref, keep_ref, send_ref):
    refs = (a_ref, b_ref, c_ref, d_ref)
    lses = []
    for ref in refs:
        tail = ref[HD:, :].astype(F32)
        lses.append(tail[0:1] + tail[1:2] + tail[2:3])
    top = functools.reduce(jnp.maximum, lses)
    ws = [jnp.exp2(lse - top) for lse in lses]
    inv = 1.0 / sum(ws)
    acc = sum(ref[:HD, :].astype(F32) * (w * inv) for ref, w in zip(refs, ws))
    left, right = acc[:, :BLK].astype(BF), acc[:, BLK:].astype(BF)

    @pl.when(where_ref[3] == 0)
    def _():
        keep_ref[...] = left
        send_ref[...] = right

    @pl.when(where_ref[3] == 1)
    def _():
        keep_ref[...] = right
        send_ref[...] = left


def project_kernel(where_ref, own_ref, other_ref, w_ref, *refs):
    out_refs, lhs_ref = refs[:4], refs[4]

    @pl.when(pl.program_id(0) == 0)
    def _():
        own, other = own_ref[...].T, other_ref[...].T

        @pl.when(where_ref[3] == 0)
        def _():
            lhs_ref[:, :HD] = own
            lhs_ref[:, HD:] = other

        @pl.when(where_ref[3] == 1)
        def _():
            lhs_ref[:, :HD] = other
            lhs_ref[:, HD:] = own

    out = jnp.dot(lhs_ref[...], w_ref[...], preferred_element_type=F32).astype(BF)
    for p in range(NY):
        out_refs[p][...] = out[p * 32 : (p + 1) * 32]


def pass_kernel(next_ref, prev_ref, a_ref, b_ref, to_next_ref, to_prev_ref):
    half = a_ref.shape[1]
    to_next_ref[...] = (next_ref[:, :half].astype(F32) + a_ref[...].astype(F32)).astype(BF)
    to_prev_ref[...] = (prev_ref[:, half:].astype(F32) + b_ref[...].astype(F32)).astype(BF)


def sum_kernel(own_ref, a_ref, b_ref, c_ref, d_ref, out_ref):
    half = a_ref.shape[1]
    own = own_ref[...].astype(F32)
    left = own[:, :half] + a_ref[...].astype(F32) + b_ref[...].astype(F32)
    right = own[:, half:] + c_ref[...].astype(F32) + d_ref[...].astype(F32)
    out_ref[:, :half] = left.astype(BF)
    out_ref[:, half:] = right.astype(BF)


def shape(*dims, dtype=BF):
    return jax.ShapeDtypeStruct(dims, dtype)


def body(queries, keys, values, block_mask, out_weight):
    where = jnp.stack([lax.axis_index(a) for a in AXES]).astype(jnp.int32)
    core = lax.axis_index("c")
    seen = jnp.pad(block_mask[:, 0, :].astype(BF), ((0, 0), (0, 64)))
    own_mask = jnp.broadcast_to(lax.dynamic_slice_in_dim(seen, core, 1), (16, 128))
    send_mask = jnp.broadcast_to(lax.dynamic_slice_in_dim(seen, 1 - core, 1), (16, 128))
    other_mask = moved(send_mask, "c", 1)

    packed = pl.pallas_call(
        prep_kernel,
        out_shape=shape(8, 32, 384),
        in_specs=[pl.BlockSpec(memory_space=pl.ANY)] * 3,
        out_specs=VMEM,
        scratch_shapes=[pltpu.VMEM((3, 32, 1024), BF), pltpu.SemaphoreType.DMA((3,))],
        compiler_params=pltpu.CompilerParams(vmem_limit_bytes=60 * 2**20),
    )(queries, keys, values)
    got = lax.all_to_all(packed, ("c", "y"), split_axis=0, concat_axis=0, tiled=True)
    q, kv = pl.pallas_call(
        mid_kernel,
        out_shape=(shape(272, HD), shape(256, 256)),
        in_specs=[SMEM] + [VMEM] * 3,
        out_specs=(VMEM, VMEM),
        compiler_params=PARAMS,
    )(where, got, own_mask, other_mask)

    pair = moved(kv, "zl", 1)
    near = [moved(kv, "x", k) for k in (1, 3, 2)]
    far = [moved(pair, "x", k) for k in (1, 3, 2)]
    kvs = [kv, near[0], near[2], near[1], pair, far[0], far[2], far[1]]
    mate = moved(q, "c", 1)
    first = moved_by_core(jnp.concatenate([q, mate]), "zh")
    across = moved_by_core(first[:272], "zh")
    second = moved(first[272:], "c", 1)
    qs = [q, first, across, second]

    parts = pl.pallas_call(
        attend_kernel,
        out_shape=tuple(shape(144, 256) for _ in range(4)),
        in_specs=[SMEM] + [VMEM] * 12,
        out_specs=(VMEM,) * 4,
        scratch_shapes=[
            pltpu.VMEM((HD, 2048), BF),
            pltpu.VMEM((2, 2048, 256), F32),
            pltpu.VMEM((2, 2048, 256), BF),
            pltpu.VMEM((HD, 1024), F32),
        ],
        compiler_params=PARAMS,
        cost_estimate=pl.CostEstimate(
            flops=2 * 2 * 1024 * 2048 * HD, bytes_accessed=2**21, transcendentals=2**21
        ),
    )(where, *qs, *kvs)
    own, plus, minus, across = parts
    back = [own, moved(across, "zh", 2), moved(plus, "zh", 1), moved(minus, "zh", -1)]

    keep, send = pl.pallas_call(
        merge_kernel,
        out_shape=(shape(HD, BLK), shape(HD, BLK)),
        in_specs=[SMEM] + [VMEM] * 4,
        out_specs=(VMEM, VMEM),
        compiler_params=PARAMS,
    )(where, *back)
    other = moved(send, "c", 1)

    cols = 1280
    width = out_weight.shape[1]
    pieces = pl.pallas_call(
        project_kernel,
        out_shape=tuple(shape(32, width) for _ in range(4)),
        grid=(width // cols,),
        in_specs=[
            SMEM,
            pl.BlockSpec((HD, BLK), lambda i: (0, 0)),
            pl.BlockSpec((HD, BLK), lambda i: (0, 0)),
            pl.BlockSpec((2 * HD, cols), lambda i: (0, i)),
        ],
        out_specs=tuple(pl.BlockSpec((32, cols), lambda i: (0, i)) for _ in range(4)),
        scratch_shapes=[pltpu.VMEM((BLK, 2 * HD), BF)],
        compiler_params=PARAMS,
        cost_estimate=pl.CostEstimate(
            flops=2 * 128 * 256 * width, bytes_accessed=2**22, transcendentals=0
        ),
    )(where, keep, other, out_weight)
    own, to_next, across, to_prev = pieces
    half = width // 2
    a = moved(across[:, :half], "y", 1)
    b = moved(across[:, half:], "y", -1)
    right_from_prev = moved(to_next[:, half:], "y", 1)
    left_from_next = moved(to_prev[:, :half], "y", -1)
    next_sum, prev_sum = pl.pallas_call(
        pass_kernel,
        out_shape=(shape(32, half), shape(32, half)),
        in_specs=[VMEM] * 4,
        out_specs=(VMEM, VMEM),
        compiler_params=PARAMS,
    )(to_next, to_prev, a, b)
    left_from_prev = moved(next_sum, "y", 1)
    right_from_next = moved(prev_sum, "y", -1)
    return pl.pallas_call(
        sum_kernel,
        out_shape=shape(32, width),
        in_specs=[VMEM] * 5,
        out_specs=VMEM,
        compiler_params=PARAMS,
    )(own, left_from_prev, left_from_next, right_from_prev, right_from_next)


def solution(mesh):
    grid = Mesh(mesh.devices.reshape(SIZES), AXES)
    rows = P(AXES, None)
    in_specs = (rows, rows, rows, P("y", AXES[:4], None), P("y", None))
    return jax.shard_map(body, mesh=grid, in_specs=in_specs, out_specs=rows, check_vma=False)
```

```python
import functools
import math

import jax
import jax.numpy as jnp
from jax import lax
from jax.experimental import pallas as pl
from jax.experimental.pallas import tpu as pltpu
from jax.sharding import Mesh, PartitionSpec as P

HD = 128
BLK = 128
NX, NH, NL, NC, NY = 4, 4, 2, 2, 4
AXES = ("x", "zh", "zl", "c", "y")
SIZES = (NX, NH, NL, NC, NY)
BF = jnp.bfloat16
F32 = jnp.float32
SCALE2 = math.log2(math.e) / math.sqrt(HD)
NEG = -1e30
BIG = 1e30
VMEM = pl.BlockSpec(memory_space=pltpu.VMEM)
PARAMS = pltpu.CompilerParams(vmem_limit_bytes=40 * 2**20)


def moved(value, axis, by):
    size = SIZES[AXES.index(axis)]
    return lax.ppermute(value, axis, [(i, (i + by) % size) for i in range(size)])


def moved_by_core(value, axis):
    size = SIZES[AXES.index(axis)]
    pairs = []
    for i in range(size):
        pairs.append((i * 2, (i + 1) % size * 2))
        pairs.append((i * 2 + 1, (i - 1) % size * 2 + 1))
    return lax.ppermute(value, (axis, "c"), pairs)


def prep_kernel(q_ref, k_ref, v_ref, out_ref, held_ref, sem):
    copies = [
        pltpu.make_async_copy(ref, held_ref.at[i], sem.at[i])
        for i, ref in enumerate((q_ref, k_ref, v_ref))
    ]
    for copy in copies:
        copy.start()
    for i, copy in enumerate(copies):
        copy.wait()
        for c in range(NC):
            for y in range(NY):
                head, slot = 2 * y + c, c * NY + y
                mine = held_ref[i, :, head * HD : (head + 1) * HD]
                if i == 0:
                    mate = head + 1 - 2 * c
                    out_ref[slot, :, :HD] = mine
                    out_ref[slot, :, HD : 2 * HD] = held_ref[i, :, mate * HD : (mate + 1) * HD]
                else:
                    out_ref[slot, :, (i + 1) * HD : (i + 2) * HD] = mine


def mid_kernel(got_ref, local_ref, other_ref, q_ref, kv_ref):
    y, c = lax.axis_index("y"), lax.axis_index("c")
    for part in range(NC):
        for p in range(NY):
            row = (part * NY + p) * 32
            source = part * NY + lax.rem(y + p, NY)
            q_ref[row : row + 32, :] = got_ref[source, :, :HD]
            q_ref[272 + row : 304 + row, :] = got_ref[source, :, HD : 2 * HD]
            kv_ref[row : row + 32, :] = got_ref[part * NY + p, :, 2 * HD :]
    local, other = local_ref[...].astype(F32), other_ref[...].astype(F32)
    low, is_zero = lax.broadcasted_iota(jnp.int32, (16, HD), 0) < 8, c == 0
    blocks = (jnp.where(is_zero, local, other), jnp.where(is_zero, other, local))
    for head in range(2):
        rows = slice(head * 8, head * 8 + 1)
        marks = jnp.where(low, blocks[0][rows], blocks[1][rows]).astype(BF)
        pl.when(c == head)(functools.partial(q_ref.__setitem__, slice(256, 272), marks))
        pl.when(c != head)(functools.partial(q_ref.__setitem__, slice(528, 544), marks))


def attend_kernel(*refs):
    q_refs, kv_refs = refs[:4], refs[4:12]
    own_ref, plus_ref, minus_ref, across_ref = refs[12:16]
    vt_ref, s_ref, p_ref, open_ref = refs[16:]
    x, zh, zl, core = (lax.axis_index(a) for a in ("x", "zh", "zl", "c"))
    for i in range(8):
        vt_ref[:, i * 256 : (i + 1) * 256] = kv_refs[i][:, HD:].T
    masks = jnp.concatenate([ref[256:272, :] for ref in q_refs], axis=0)
    row = lax.broadcasted_iota(jnp.int32, (64, 1024), 0)
    block = lax.broadcasted_iota(jnp.int32, (64, 1024), 1) // BLK
    pick = jnp.where(row == block * 8, 1.0, 0.0).astype(BF)
    open_ref[...] = lax.dot_general(
        masks, pick, (((0,), (0,)), ((), ())), preferred_element_type=F32
    )

    def score(j):
        q = q_refs[j][:256, :]
        opens = []
        top = jnp.full((1, 256), NEG, F32)
        for i in range(8):
            step, flip = i % 4, i // 4
            source = lax.rem(x + NX - step, NX) * 16 + zh * 4 + lax.rem(zl + flip, 2) * 2
            s = lax.dot_general(
                kv_refs[i][:, :HD], q, (((1,), (1,)), ((), ())), preferred_element_type=F32
            )
            s_ref[j % 2, i * 256 : (i + 1) * 256, :] = s
            for part in range(2):
                is_open = open_ref[pl.ds(source + part, 1), j * 256 : (j + 1) * 256] > 0.5
                opens.append(is_open)
                here = jnp.max(s[part * BLK : (part + 1) * BLK], axis=0, keepdims=True)
                top = jnp.maximum(top, jnp.where(is_open, here, NEG))
        return opens, top * SCALE2

    following = score(0)
    for j in range(4):
        opens, top = following
        if j < 3:
            following = score(j + 1)
        sums = jnp.zeros((8, 256), F32)
        for b in range(16):
            less = jnp.where(opens[b], top, BIG)
            rows = slice(b * BLK, (b + 1) * BLK)
            w = jnp.exp2(s_ref[j % 2, rows, :] * SCALE2 - less)
            sums += jnp.sum(w.reshape(16, 8, 256), axis=0)
            p_ref[j % 2, rows, :] = w.astype(BF)
        total = jnp.sum(sums, axis=0, keepdims=True)
        acc = jnp.dot(vt_ref[...], p_ref[j % 2], preferred_element_type=F32)
        some = total > 0.0
        safe = jnp.where(some, total, 1.0)
        out = (acc / safe).astype(BF)
        lse = jnp.where(some, top + jnp.log2(safe), NEG)
        hi = lse.astype(BF).astype(F32)
        mid = (lse - hi).astype(BF).astype(F32)
        low = lse - hi - mid
        row = lax.broadcasted_iota(jnp.int32, (16, 256), 0)
        tail = jnp.where(row == 0, hi, jnp.where(row == 1, mid, low)).astype(BF)

        def put(ref, out=out, tail=tail):
            ref[:HD, :] = out
            ref[HD:, :] = tail

        if j == 0:
            put(own_ref)
        elif j == 2:
            put(across_ref)
        else:
            pl.when(core == (j == 3))(functools.partial(put, minus_ref))
            pl.when(core != (j == 3))(functools.partial(put, plus_ref))


def merge_kernel(a_ref, b_ref, c_ref, d_ref, keep_ref, send_ref):
    refs = (a_ref, b_ref, c_ref, d_ref)
    lses = []
    for ref in refs:
        tail = ref[HD:, :].astype(F32)
        lses.append(tail[0:1] + tail[1:2] + tail[2:3])
    top = functools.reduce(jnp.maximum, lses)
    ws = [jnp.exp2(lse - top) for lse in lses]
    inv = 1.0 / sum(ws)
    acc = sum(ref[:HD, :].astype(F32) * (w * inv) for ref, w in zip(refs, ws))
    left, right = acc[:, :BLK].astype(BF), acc[:, BLK:].astype(BF)

    @pl.when(lax.axis_index("c") == 0)
    def _():
        keep_ref[...] = left
        send_ref[...] = right

    @pl.when(lax.axis_index("c") == 1)
    def _():
        keep_ref[...] = right
        send_ref[...] = left


def project_kernel(own_ref, other_ref, w_ref, *refs):
    out_refs, lhs_ref = refs[:4], refs[4]

    @pl.when(pl.program_id(0) == 0)
    def _():
        own, other = own_ref[...].T, other_ref[...].T

        @pl.when(lax.axis_index("c") == 0)
        def _():
            lhs_ref[:, :HD] = own
            lhs_ref[:, HD:] = other

        @pl.when(lax.axis_index("c") == 1)
        def _():
            lhs_ref[:, :HD] = other
            lhs_ref[:, HD:] = own

    out = jnp.dot(lhs_ref[...], w_ref[...], preferred_element_type=F32).astype(BF)
    for p in range(NY):
        out_refs[p][...] = out[p * 32 : (p + 1) * 32]


def pass_kernel(next_ref, prev_ref, a_ref, b_ref, to_next_ref, to_prev_ref):
    half = a_ref.shape[1]
    to_next_ref[...] = (next_ref[:, :half].astype(F32) + a_ref[...].astype(F32)).astype(BF)
    to_prev_ref[...] = (prev_ref[:, half:].astype(F32) + b_ref[...].astype(F32)).astype(BF)


def sum_kernel(own_ref, a_ref, b_ref, c_ref, d_ref, out_ref):
    half = a_ref.shape[1]
    own = own_ref[...].astype(F32)
    left = own[:, :half] + a_ref[...].astype(F32) + b_ref[...].astype(F32)
    right = own[:, half:] + c_ref[...].astype(F32) + d_ref[...].astype(F32)
    out_ref[:, :half] = left.astype(BF)
    out_ref[:, half:] = right.astype(BF)


def shape(*dims, dtype=BF):
    return jax.ShapeDtypeStruct(dims, dtype)


def body(queries, keys, values, block_mask, out_weight):
    seen = jnp.pad(block_mask[:, 0, :].astype(BF), ((0, 0), (0, 64)))
    local = jnp.repeat(seen, 8, axis=0)
    other = moved(local, "c", 1)

    packed = pl.pallas_call(
        prep_kernel,
        out_shape=shape(8, 32, 512),
        in_specs=[pl.BlockSpec(memory_space=pl.ANY)] * 3,
        out_specs=VMEM,
        scratch_shapes=[pltpu.VMEM((3, 32, 1024), BF), pltpu.SemaphoreType.DMA((3,))],
        compiler_params=pltpu.CompilerParams(vmem_limit_bytes=60 * 2**20),
    )(queries, keys, values)
    got = lax.all_to_all(packed, ("c", "y"), split_axis=0, concat_axis=0, tiled=True)
    q, kv = pl.pallas_call(
        mid_kernel,
        out_shape=(shape(544, HD), shape(256, 256)),
        in_specs=[VMEM] * 3,
        out_specs=(VMEM, VMEM),
        compiler_params=PARAMS,
    )(got, local, other)

    pair = moved(kv, "zl", 1)
    near = [moved(kv, "x", k) for k in (1, 3, 2)]
    far = [moved(pair, "x", k) for k in (1, 3, 2)]
    kvs = [kv, near[0], near[2], near[1], pair, far[0], far[2], far[1]]
    first = moved_by_core(q, "zh")
    across = moved_by_core(first[:272], "zh")
    second = moved(first[272:], "c", 1)
    qs = [q, first, across, second]

    parts = pl.pallas_call(
        attend_kernel,
        out_shape=tuple(shape(144, 256) for _ in range(4)),
        in_specs=[VMEM] * 12,
        out_specs=(VMEM,) * 4,
        scratch_shapes=[
            pltpu.VMEM((HD, 2048), BF),
            pltpu.VMEM((2, 2048, 256), F32),
            pltpu.VMEM((2, 2048, 256), BF),
            pltpu.VMEM((HD, 1024), F32),
        ],
        compiler_params=PARAMS,
        cost_estimate=pl.CostEstimate(
            flops=2 * 2 * 1024 * 2048 * HD, bytes_accessed=2**21, transcendentals=2**21
        ),
    )(*qs, *kvs)
    own, plus, minus, across = parts
    back = [own, moved(across, "zh", 2), moved(plus, "zh", 1), moved(minus, "zh", -1)]

    keep, send = pl.pallas_call(
        merge_kernel,
        out_shape=(shape(HD, BLK), shape(HD, BLK)),
        in_specs=[VMEM] * 4,
        out_specs=(VMEM, VMEM),
        compiler_params=PARAMS,
    )(*back)
    other = moved(send, "c", 1)

    cols = 1280
    width = out_weight.shape[1]
    pieces = pl.pallas_call(
        project_kernel,
        out_shape=tuple(shape(32, width) for _ in range(4)),
        grid=(width // cols,),
        in_specs=[
            pl.BlockSpec((HD, BLK), lambda i: (0, 0)),
            pl.BlockSpec((HD, BLK), lambda i: (0, 0)),
            pl.BlockSpec((2 * HD, cols), lambda i: (0, i)),
        ],
        out_specs=tuple(pl.BlockSpec((32, cols), lambda i: (0, i)) for _ in range(4)),
        scratch_shapes=[pltpu.VMEM((BLK, 2 * HD), BF)],
        compiler_params=PARAMS,
        cost_estimate=pl.CostEstimate(
            flops=2 * 128 * 256 * width, bytes_accessed=2**22, transcendentals=0
        ),
    )(keep, other, out_weight)
    own, to_next, across, to_prev = pieces
    half = width // 2
    a = moved(across[:, :half], "y", 1)
    b = moved(across[:, half:], "y", -1)
    right_from_prev = moved(to_next[:, half:], "y", 1)
    left_from_next = moved(to_prev[:, :half], "y", -1)
    next_sum, prev_sum = pl.pallas_call(
        pass_kernel,
        out_shape=(shape(32, half), shape(32, half)),
        in_specs=[VMEM] * 4,
        out_specs=(VMEM, VMEM),
        compiler_params=PARAMS,
    )(to_next, to_prev, a, b)
    left_from_prev = moved(next_sum, "y", 1)
    right_from_next = moved(prev_sum, "y", -1)
    return pl.pallas_call(
        sum_kernel,
        out_shape=shape(32, width),
        in_specs=[VMEM] * 5,
        out_specs=VMEM,
        compiler_params=PARAMS,
    )(own, left_from_prev, left_from_next, right_from_prev, right_from_next)


def solution(mesh):
    grid = Mesh(mesh.devices.reshape(SIZES), AXES)
    rows = P(AXES, None)
    in_specs = (rows, rows, rows, P("y", AXES[:4], None), P("y", None))
    return jax.shard_map(body, mesh=grid, in_specs=in_specs, out_specs=rows, check_vma=False)
```

```python
import functools
import math

import jax
import jax.numpy as jnp
from jax import lax
from jax.experimental import pallas as pl
from jax.experimental.pallas import tpu as pltpu
from jax.sharding import Mesh, PartitionSpec as P

HD = 128
BLK = 128
NX, NH, NL, NC, NY = 4, 4, 2, 2, 4
AXES = ("x", "zh", "zl", "c", "y")
SIZES = (NX, NH, NL, NC, NY)
BF = jnp.bfloat16
F32 = jnp.float32
SCALE2 = math.log2(math.e) / math.sqrt(HD)
NEG = -1e30
BIG = 1e30
VMEM = pl.BlockSpec(memory_space=pltpu.VMEM)
PARAMS = pltpu.CompilerParams(vmem_limit_bytes=40 * 2**20)


def moved(value, axis, by):
    size = SIZES[AXES.index(axis)]
    return lax.ppermute(value, axis, [(i, (i + by) % size) for i in range(size)])


def swapped(value, axis, mask):
    size = SIZES[AXES.index(axis)]
    return lax.ppermute(value, axis, [(i, i ^ mask) for i in range(size)])


def swapped_by_core(value, axis, masks):
    size = SIZES[AXES.index(axis)]
    pairs = [(i * NC + c, (i ^ masks[c]) * NC + c) for i in range(size) for c in range(NC)]
    return lax.ppermute(value, (axis, "c"), pairs)


def prep_kernel(q_ref, k_ref, v_ref, mask_ref, *refs):
    out_refs, marks_ref, held_ref, seen_ref, sem = refs[:4], *refs[4:]
    y, c = lax.axis_index("y"), lax.axis_index("c")
    copies = [
        pltpu.make_async_copy(ref, held_ref.at[i], sem.at[i])
        for i, ref in enumerate((q_ref, k_ref, v_ref))
    ]
    copies.append(pltpu.make_async_copy(mask_ref, seen_ref, sem.at[3]))
    for copy in copies:
        copy.start()
    copies.pop().wait()
    seen = seen_ref[:, 0, :].astype(F32)
    seen = jnp.concatenate([seen, jnp.zeros_like(seen)], axis=1)
    low = lax.broadcasted_iota(jnp.int32, (16, HD), 0) < 8
    marks_ref[...] = jnp.where(low, seen[0:1], seen[1:2]).astype(BF)
    for i, copy in enumerate(copies):
        copy.wait()
        for mask, out_ref in enumerate(out_refs):
            for mate in range(2):
                head = (y ^ mask) * 2 + (c ^ mate)
                cols = pl.ds(pl.multiple_of(head * HD, HD), HD)
                slot = mate if i == 0 else 1 + 2 * mate + i
                out_ref[:, slot * HD : (slot + 1) * HD] = held_ref[i, :, cols]


def pack_kernel(marks_ref, *refs):
    piece_refs, (mine_ref, send_ref) = refs[:4], refs[4:]
    for mask, ref in enumerate(piece_refs):
        rows = slice(mask * 32, (mask + 1) * 32)
        mine_ref[rows, :] = ref[:, : 4 * HD]
        send_ref[rows, :HD] = ref[:, HD : 2 * HD]
        send_ref[rows, HD : 2 * HD] = ref[:, :HD]
        send_ref[rows, 2 * HD :] = ref[:, 4 * HD :]
    for ref in (mine_ref, send_ref):
        for slot in range(4):
            ref[BLK:, slot * HD : (slot + 1) * HD] = marks_ref[...]


def mid_kernel(mine_ref, got_ref, q_ref, kv_ref):
    for core in range(NC):

        @pl.when(lax.axis_index("c") == core)
        def _():
            for part, ref in enumerate((mine_ref, got_ref)):
                row = (core ^ part) * BLK
                q_ref[row : row + BLK, :] = ref[:BLK, :HD]
                q_ref[272 + row : 272 + row + BLK, :] = ref[:BLK, HD : 2 * HD]
                kv_ref[row : row + BLK, :] = ref[:BLK, 2 * HD :]
            marks = [ref[BLK:, :HD].astype(F32) for ref in (mine_ref, got_ref)]
            low = lax.broadcasted_iota(jnp.int32, (16, HD), 0) < 8
            for mate in range(2):
                row = (core ^ mate) * 8
                both = [marks[core][row : row + 1], marks[1 - core][row : row + 1]]
                q_ref[256 + 272 * mate : 272 + 272 * mate, :] = jnp.where(low, *both).astype(BF)


def attend_kernel(count, merging, *refs):
    q_refs, kv_refs = refs[:count], refs[count : count + 8]
    met_ref = refs[count + 8] if merging else None
    refs = refs[count + 8 + merging :]
    out_refs, (vt_ref, s_ref, p_ref, open_ref) = refs[:count], refs[count:]
    x, zh, zl = (lax.axis_index(a) for a in ("x", "zh", "zl"))
    for i in range(8):
        vt_ref[:, i * 256 : (i + 1) * 256] = kv_refs[i][:, HD:].T
    masks = [ref[256:272, :] for ref in q_refs]
    masks = jnp.concatenate(masks, axis=0) if count > 1 else masks[0]
    row = lax.broadcasted_iota(jnp.int32, (16 * count, 256 * count), 0)
    block = lax.broadcasted_iota(jnp.int32, (16 * count, 256 * count), 1) // BLK
    pick = jnp.where(row == block * 8, 1.0, 0.0).astype(BF)
    open_ref[...] = lax.dot_general(
        masks, pick, (((0,), (0,)), ((), ())), preferred_element_type=F32
    )

    def score(j):
        q = q_refs[j][:256, :]
        opens = []
        top = jnp.full((1, 256), NEG, F32)
        for i in range(8):
            source = (x ^ (i % 4)) * 16 + zh * 4 + (zl ^ (i // 4)) * 2
            s = lax.dot_general(
                kv_refs[i][:, :HD], q, (((1,), (1,)), ((), ())), preferred_element_type=F32
            )
            s_ref[j % 2, i * 256 : (i + 1) * 256, :] = s
            for part in range(2):
                is_open = open_ref[pl.ds(source + part, 1), j * 256 : (j + 1) * 256] > 0.5
                opens.append(is_open)
                here = jnp.max(s[part * BLK : (part + 1) * BLK], axis=0, keepdims=True)
                top = jnp.maximum(top, jnp.where(is_open, here, NEG))
        return opens, top * SCALE2

    following = score(0)
    for j in range(count):
        opens, top = following
        if j < count - 1:
            following = score(j + 1)
        sums = jnp.zeros((8, 256), F32)
        for b in range(16):
            less = jnp.where(opens[b], top, BIG)
            rows = slice(b * BLK, (b + 1) * BLK)
            w = jnp.exp2(s_ref[j % 2, rows, :] * SCALE2 - less)
            sums += jnp.sum(w.reshape(16, 8, 256), axis=0)
            p_ref[j % 2, rows, :] = w.astype(BF)
        total = jnp.sum(sums, axis=0, keepdims=True)
        acc = jnp.dot(vt_ref[...], p_ref[j % 2], preferred_element_type=F32)
        some = total > 0.0
        safe = jnp.where(some, total, 1.0)
        acc = acc / safe
        lse = jnp.where(some, top + jnp.log2(safe), NEG)
        if merging:
            tail = met_ref[HD:, :].astype(F32)
            met = tail[0:1] + tail[1:2] + tail[2:3]
            top = jnp.maximum(lse, met)
            mine, theirs = jnp.exp2(lse - top), jnp.exp2(met - top)
            total = mine + theirs
            acc = acc * (mine / total) + met_ref[:HD, :].astype(F32) * (theirs / total)
            lse = top + jnp.log2(total)
        out_refs[j][:HD, :] = acc.astype(BF)
        out_refs[j][HD:, :] = packed_tail(lse)


def packed_tail(lse):
    hi = lse.astype(BF).astype(F32)
    mid = (lse - hi).astype(BF).astype(F32)
    row = lax.broadcasted_iota(jnp.int32, (16, lse.shape[1]), 0)
    return jnp.where(row == 0, hi, jnp.where(row == 1, mid, lse - hi - mid)).astype(BF)


def merged(parts):
    lses = []
    for part in parts:
        tail = part[HD:, :].astype(F32)
        lses.append(tail[0:1] + tail[1:2] + tail[2:3])
    top = functools.reduce(jnp.maximum, lses)
    ws = [jnp.exp2(lse - top) for lse in lses]
    total = sum(ws)
    inv = 1.0 / total
    acc = sum(part[:HD, :].astype(F32) * (w * inv) for part, w in zip(parts, ws))
    return acc.astype(BF), top + jnp.log2(total)


def join_kernel(a_ref, b_ref, out_ref):
    out_ref[:144, :] = a_ref[...]
    out_ref[144:, :] = b_ref[...]


def share_kernel(own_ref, side_ref, send_ref):
    for core in range(NC):

        @pl.when(lax.axis_index("c") == core)
        def _():
            cols = slice((1 - core) * BLK, (2 - core) * BLK)
            acc, lse = merged([own_ref[:, cols], side_ref[:144, cols]])
            send_ref[:HD, :] = acc
            send_ref[HD:144, :] = packed_tail(lse)
            send_ref[144:, :] = side_ref[144:, cols]


def project_kernel(own_ref, side_ref, got_ref, w_ref, *refs):
    out_refs, lhs_ref = refs[:4], refs[4]
    for core in range(NC):

        @pl.when(lax.axis_index("c") == core)
        def _():
            cols = slice(core * BLK, (core + 1) * BLK)
            mine = [own_ref[:, cols], side_ref[:144, cols], got_ref[144:]]
            mate = [side_ref[144:, cols], got_ref[:144]]
            lhs_ref[:, core * HD : (core + 1) * HD] = merged(mine)[0].T
            lhs_ref[:, (1 - core) * HD : (2 - core) * HD] = merged(mate)[0].T

    lhs = lhs_ref[...]
    for start in range(0, w_ref.shape[1], 512):
        cols = slice(start, start + 512)
        out = jnp.dot(lhs, w_ref[:, cols], preferred_element_type=F32).astype(BF)
        for p in range(NY):
            out_refs[p][:, cols] = out[p * 32 : (p + 1) * 32]


def pass_kernel(one_ref, three_ref, a_ref, b_ref, by_one_ref, by_three_ref):
    half = a_ref.shape[1]
    by_one_ref[...] = (one_ref[:, half:].astype(F32) + b_ref[...].astype(F32)).astype(BF)
    by_three_ref[...] = (three_ref[:, :half].astype(F32) + a_ref[...].astype(F32)).astype(BF)


def sum_kernel(own_ref, a_ref, b_ref, c_ref, d_ref, out_ref, total_ref, sem):
    half = a_ref.shape[1]
    step = half // 2
    copies = []
    for i, (one, two) in enumerate(((c_ref, d_ref), (a_ref, b_ref))):
        base = half * (1 - i)
        for start in range(0, half, step):
            cols = slice(start, start + step)
            spot = slice(base + start, base + start + step)
            total = own_ref[:, spot].astype(F32) + one[:, cols].astype(F32)
            total_ref[:, spot] = (total + two[:, cols].astype(F32)).astype(BF)
            there = out_ref.at[:, pl.ds(base + start, step)]
            here = total_ref.at[:, pl.ds(base + start, step)]
            copies.append(pltpu.make_async_copy(here, there, sem.at[len(copies)]))
            copies[-1].start()
    for copy in copies:
        copy.wait()


def shape(*dims, dtype=BF):
    return jax.ShapeDtypeStruct(dims, dtype)


def attend(qs, kvs, met=None):
    count, merging = len(qs), met is not None
    return pl.pallas_call(
        functools.partial(attend_kernel, count, merging),
        out_shape=tuple(shape(144, 256) for _ in range(count)),
        in_specs=[VMEM] * (count + 8 + merging),
        out_specs=(VMEM,) * count,
        scratch_shapes=[
            pltpu.VMEM((HD, 2048), BF),
            pltpu.VMEM((2, 2048, 256), F32),
            pltpu.VMEM((2, 2048, 256), BF),
            pltpu.VMEM((HD, 256 * count), F32),
        ],
        compiler_params=PARAMS,
        cost_estimate=pl.CostEstimate(
            flops=2 * 2 * 256 * count * 2048 * HD * 8,
            bytes_accessed=2**21,
            transcendentals=2**19 * count,
        ),
    )(*qs, *kvs, *([met] if merging else []))


def body(queries, keys, values, block_mask, out_weight):
    *pieces, marks = pl.pallas_call(
        prep_kernel,
        out_shape=tuple(shape(32, 768) for _ in range(4)) + (shape(16, HD),),
        in_specs=[pl.BlockSpec(memory_space=pl.ANY)] * 4,
        out_specs=(VMEM,) * 5,
        scratch_shapes=[
            pltpu.VMEM((3, 32, 1024), BF),
            pltpu.VMEM(block_mask.shape, jnp.int32),
            pltpu.SemaphoreType.DMA((4,)),
        ],
        compiler_params=PARAMS,
    )(*(pltpu.with_memory_space_constraint(t, pltpu.HBM) for t in (queries, keys, values, block_mask)))
    met = {m: swapped(pieces[m], "y", m) for m in (2, 3, 1)}
    mine, send = pl.pallas_call(
        pack_kernel,
        out_shape=(shape(144, 512), shape(144, 512)),
        in_specs=[VMEM] * 5,
        out_specs=(VMEM, VMEM),
        compiler_params=PARAMS,
    )(marks, pieces[0], met[1], met[2], met[3])
    got = moved(send, "c", 1)
    q, kv = pl.pallas_call(
        mid_kernel,
        out_shape=(shape(544, HD), shape(256, 256)),
        in_specs=[VMEM] * 2,
        out_specs=(VMEM, VMEM),
        compiler_params=PARAMS,
    )(mine, got)

    pair = swapped(kv, "zl", 1)
    near = [swapped(kv, "x", m) for m in (1, 3, 2)]
    far = [swapped(pair, "x", m) for m in (1, 3, 2)]
    kvs = [kv, near[0], near[2], near[1], pair, far[0], far[2], far[1]]
    first = swapped_by_core(q, "zh", (1, 3))
    across = swapped_by_core(first[:272], "zh", (3, 1))
    second = moved(first[272:], "c", 1)
    qs = [q, first, across, second]

    across, give = attend((across, first), kvs)
    across = swapped(across, "zh", 2)
    took = moved(give, "c", 1)
    (keep,) = attend((second,), kvs)
    joined = pl.pallas_call(
        join_kernel,
        out_shape=shape(288, 256),
        in_specs=[VMEM] * 2,
        out_specs=VMEM,
        compiler_params=PARAMS,
    )(keep, took)
    side = swapped_by_core(joined, "zh", (3, 1))
    (own,) = attend((q,), kvs, across)
    send = pl.pallas_call(
        share_kernel,
        out_shape=shape(288, BLK),
        in_specs=[VMEM] * 2,
        out_specs=VMEM,
        compiler_params=PARAMS,
    )(own, side)
    got = moved(send, "c", 1)

    width = out_weight.shape[1]
    pieces = pl.pallas_call(
        project_kernel,
        out_shape=tuple(shape(32, width) for _ in range(4)),
        in_specs=[VMEM] * 4,
        out_specs=(VMEM,) * 4,
        scratch_shapes=[pltpu.VMEM((BLK, 2 * HD), BF)],
        compiler_params=PARAMS,
        cost_estimate=pl.CostEstimate(
            flops=2 * 128 * 256 * width, bytes_accessed=2**22, transcendentals=0
        ),
    )(own, side, got, out_weight)
    own, one, two, three = pieces
    half = width // 2
    b = swapped(two[:, half:], "y", 3)
    a = swapped(two[:, :half], "y", 1)
    right_three = swapped(three[:, half:], "y", 3)
    left_one = swapped(one[:, :half], "y", 1)
    by_one, by_three = pl.pallas_call(
        pass_kernel,
        out_shape=(shape(32, half), shape(32, half)),
        in_specs=[VMEM] * 4,
        out_specs=(VMEM, VMEM),
        compiler_params=PARAMS,
    )(one, three, a, b)
    left_three = swapped(by_three, "y", 3)
    right_one = swapped(by_one, "y", 1)
    return pl.pallas_call(
        sum_kernel,
        out_shape=shape(32, width),
        in_specs=[VMEM] * 5,
        out_specs=pl.BlockSpec(memory_space=pl.ANY),
        scratch_shapes=[pltpu.VMEM((32, width), BF), pltpu.SemaphoreType.DMA((4,))],
        compiler_params=PARAMS,
    )(own, left_one, left_three, right_one, right_three)


def solution(mesh):
    grid = Mesh(mesh.devices.reshape(SIZES), AXES)
    rows = P(AXES, None)
    in_specs = (rows, rows, rows, P("y", AXES[:4], None), P("y", None))
    return jax.shard_map(body, mesh=grid, in_specs=in_specs, out_specs=rows, check_vma=False)
```

```python
import functools
import math

import jax
import jax.numpy as jnp
from jax import lax
from jax.experimental import pallas as pl
from jax.experimental.pallas import tpu as pltpu
from jax.sharding import Mesh, PartitionSpec as P

HD = 128
BLK = 128
NX, NH, NL, NC, NY = 4, 4, 2, 2, 4
AXES = ("x", "zh", "zl", "c", "y")
SIZES = (NX, NH, NL, NC, NY)
BF = jnp.bfloat16
F32 = jnp.float32
SCALE2 = math.log2(math.e) / math.sqrt(HD)
NEG = -1e30
BIG = 1e30
VMEM = pl.BlockSpec(memory_space=pltpu.VMEM)
PARAMS = pltpu.CompilerParams(vmem_limit_bytes=40 * 2**20)


def moved(value, axis, by):
    size = SIZES[AXES.index(axis)]
    return lax.ppermute(value, axis, [(i, (i + by) % size) for i in range(size)])


def swapped(value, axis, mask):
    size = SIZES[AXES.index(axis)]
    return lax.ppermute(value, axis, [(i, i ^ mask) for i in range(size)])


def swapped_by_core(value, axis, masks):
    size = SIZES[AXES.index(axis)]
    pairs = [(i * NC + c, (i ^ masks[c]) * NC + c) for i in range(size) for c in range(NC)]
    return lax.ppermute(value, (axis, "c"), pairs)


def prep_kernel(q_ref, k_ref, v_ref, mask_ref, *refs):
    out_refs, marks_ref, held_ref, seen_ref, sem = refs[:4], *refs[4:]
    y, c = lax.axis_index("y"), lax.axis_index("c")
    copies = [
        pltpu.make_async_copy(ref, held_ref.at[i], sem.at[i])
        for i, ref in enumerate((q_ref, k_ref, v_ref))
    ]
    copies.append(pltpu.make_async_copy(mask_ref, seen_ref, sem.at[3]))
    for copy in copies:
        copy.start()
    copies.pop().wait()
    seen = seen_ref[:, 0, :].astype(F32)
    seen = jnp.concatenate([seen, jnp.zeros_like(seen)], axis=1)
    low = lax.broadcasted_iota(jnp.int32, (16, HD), 0) < 8
    marks_ref[...] = jnp.where(low, seen[0:1], seen[1:2]).astype(BF)
    for i, copy in enumerate(copies):
        copy.wait()
        for mask, out_ref in enumerate(out_refs):
            for mate in range(2):
                head = (y ^ mask) * 2 + (c ^ mate)
                cols = pl.ds(pl.multiple_of(head * HD, HD), HD)
                slot = mate if i == 0 else 1 + 2 * mate + i
                out_ref[:, slot * HD : (slot + 1) * HD] = held_ref[i, :, cols]


def pack_kernel(marks_ref, *refs):
    piece_refs, (mine_ref, send_ref) = refs[:4], refs[4:]
    for mask, ref in enumerate(piece_refs):
        rows = slice(mask * 32, (mask + 1) * 32)
        mine_ref[rows, :] = ref[:, : 4 * HD]
        send_ref[rows, :HD] = ref[:, HD : 2 * HD]
        send_ref[rows, HD : 2 * HD] = ref[:, :HD]
        send_ref[rows, 2 * HD :] = ref[:, 4 * HD :]
    for ref in (mine_ref, send_ref):
        for slot in range(4):
            ref[BLK:, slot * HD : (slot + 1) * HD] = marks_ref[...]


def mid_kernel(mine_ref, got_ref, q_ref, kv_ref):
    for core in range(NC):

        @pl.when(lax.axis_index("c") == core)
        def _():
            for part, ref in enumerate((mine_ref, got_ref)):
                row = (core ^ part) * BLK
                q_ref[row : row + BLK, :] = ref[:BLK, :HD]
                q_ref[272 + row : 272 + row + BLK, :] = ref[:BLK, HD : 2 * HD]
                kv_ref[row : row + BLK, :] = ref[:BLK, 2 * HD :]
            marks = [ref[BLK:, :HD].astype(F32) for ref in (mine_ref, got_ref)]
            low = lax.broadcasted_iota(jnp.int32, (16, HD), 0) < 8
            for mate in range(2):
                row = (core ^ mate) * 8
                both = [marks[core][row : row + 1], marks[1 - core][row : row + 1]]
                q_ref[256 + 272 * mate : 272 + 272 * mate, :] = jnp.where(low, *both).astype(BF)


def attend_kernel(count, chunks, early, merging, *refs):
    refs = list(refs)
    q_refs = [refs.pop(0) for _ in range(count)]
    kv_refs = [refs.pop(0) for _ in chunks]
    before = [] if early else [(refs.pop(0), refs.pop(0)) for _ in range(count)]
    met_ref = refs.pop(0) if merging else None
    out_refs = [refs.pop(0) for _ in range(count * (1 + early))]
    vt_ref, s_ref, p_ref, open_ref = refs
    x, zh, zl = (lax.axis_index(a) for a in ("x", "zh", "zl"))
    for i, ref in enumerate(kv_refs):
        vt_ref[:, i * 256 : (i + 1) * 256] = ref[:, HD:].T
    masks = [ref[256:272, :] for ref in q_refs]
    masks = jnp.concatenate(masks, axis=0) if count > 1 else masks[0]
    row = lax.broadcasted_iota(jnp.int32, (16 * count, 256 * count), 0)
    block = lax.broadcasted_iota(jnp.int32, (16 * count, 256 * count), 1) // BLK
    pick = jnp.where(row == block * 8, 1.0, 0.0).astype(BF)
    open_ref[...] = lax.dot_general(
        masks, pick, (((0,), (0,)), ((), ())), preferred_element_type=F32
    )

    def score(j):
        q = q_refs[j][:256, :]
        opens = []
        top = jnp.full((1, 256), NEG, F32)
        for i, chunk in enumerate(chunks):
            source = (x ^ (chunk % 4)) * 16 + zh * 4 + (zl ^ (chunk // 4)) * 2
            s = lax.dot_general(
                kv_refs[i][:, :HD], q, (((1,), (1,)), ((), ())), preferred_element_type=F32
            )
            s_ref[j % 2, i * 256 : (i + 1) * 256, :] = s
            for part in range(2):
                is_open = open_ref[pl.ds(source + part, 1), j * 256 : (j + 1) * 256] > 0.5
                opens.append(is_open)
                here = jnp.max(s[part * BLK : (part + 1) * BLK], axis=0, keepdims=True)
                top = jnp.maximum(top, jnp.where(is_open, here, NEG))
        return opens, top * SCALE2

    following = score(0)
    for j in range(count):
        opens, top = following
        if j < count - 1:
            following = score(j + 1)
        sums = jnp.zeros((8, 256), F32)
        for b in range(2 * len(chunks)):
            less = jnp.where(opens[b], top, BIG)
            rows = slice(b * BLK, (b + 1) * BLK)
            w = jnp.exp2(s_ref[j % 2, rows, :] * SCALE2 - less)
            sums += jnp.sum(w.reshape(16, 8, 256), axis=0)
            p_ref[j % 2, rows, :] = w.astype(BF)
        total = jnp.sum(sums, axis=0, keepdims=True)
        acc = jnp.dot(vt_ref[...], p_ref[j % 2], preferred_element_type=F32)
        if early:
            row = lax.broadcasted_iota(jnp.int32, (8, 256), 0)
            out_refs[2 * j][...] = acc
            out_refs[2 * j + 1][...] = jnp.where(row == 0, top, total)
            continue
        acc_ref, stat_ref = before[j]
        top0, total0 = stat_ref[0:1, :], stat_ref[1:2, :]
        both = jnp.maximum(top, top0)
        keep, keep0 = jnp.exp2(top - both), jnp.exp2(top0 - both)
        acc = acc * keep + acc_ref[...] * keep0
        top, total = both, total * keep + total0 * keep0
        some = total > 0.0
        safe = jnp.where(some, total, 1.0)
        acc = acc / safe
        lse = jnp.where(some, top + jnp.log2(safe), NEG)
        if merging:
            tail = met_ref[HD:, :].astype(F32)
            met = tail[0:1] + tail[1:2] + tail[2:3]
            top = jnp.maximum(lse, met)
            mine, theirs = jnp.exp2(lse - top), jnp.exp2(met - top)
            total = mine + theirs
            acc = acc * (mine / total) + met_ref[:HD, :].astype(F32) * (theirs / total)
            lse = top + jnp.log2(total)
        out_refs[j][:HD, :] = acc.astype(BF)
        out_refs[j][HD:, :] = packed_tail(lse)


def packed_tail(lse):
    hi = lse.astype(BF).astype(F32)
    mid = (lse - hi).astype(BF).astype(F32)
    row = lax.broadcasted_iota(jnp.int32, (16, lse.shape[1]), 0)
    return jnp.where(row == 0, hi, jnp.where(row == 1, mid, lse - hi - mid)).astype(BF)


def merged(parts):
    lses = []
    for part in parts:
        tail = part[HD:, :].astype(F32)
        lses.append(tail[0:1] + tail[1:2] + tail[2:3])
    top = functools.reduce(jnp.maximum, lses)
    ws = [jnp.exp2(lse - top) for lse in lses]
    total = sum(ws)
    inv = 1.0 / total
    acc = sum(part[:HD, :].astype(F32) * (w * inv) for part, w in zip(parts, ws))
    return acc.astype(BF), top + jnp.log2(total)


def join_kernel(a_ref, b_ref, out_ref):
    out_ref[:144, :] = a_ref[...]
    out_ref[144:, :] = b_ref[...]


def share_kernel(own_ref, side_ref, send_ref):
    for core in range(NC):

        @pl.when(lax.axis_index("c") == core)
        def _():
            cols = slice((1 - core) * BLK, (2 - core) * BLK)
            acc, lse = merged([own_ref[:, cols], side_ref[:144, cols]])
            send_ref[:HD, :] = acc
            send_ref[HD:144, :] = packed_tail(lse)
            send_ref[144:, :] = side_ref[144:, cols]


def project_kernel(own_ref, side_ref, got_ref, w_ref, *refs):
    out_refs, lhs_ref = refs[:4], refs[4]
    for core in range(NC):

        @pl.when(lax.axis_index("c") == core)
        def _():
            cols = slice(core * BLK, (core + 1) * BLK)
            mine = [own_ref[:, cols], side_ref[:144, cols], got_ref[144:]]
            mate = [side_ref[144:, cols], got_ref[:144]]
            lhs_ref[:, core * HD : (core + 1) * HD] = merged(mine)[0].T
            lhs_ref[:, (1 - core) * HD : (2 - core) * HD] = merged(mate)[0].T

    lhs = lhs_ref[...]
    for start in range(0, w_ref.shape[1], 512):
        cols = slice(start, start + 512)
        out = jnp.dot(lhs, w_ref[:, cols], preferred_element_type=F32).astype(BF)
        for p in range(NY):
            out_refs[p][:, cols] = out[p * 32 : (p + 1) * 32]


def pass_kernel(one_ref, three_ref, a_ref, b_ref, by_one_ref, by_three_ref):
    half = a_ref.shape[1]
    by_one_ref[...] = (one_ref[:, half:].astype(F32) + b_ref[...].astype(F32)).astype(BF)
    by_three_ref[...] = (three_ref[:, :half].astype(F32) + a_ref[...].astype(F32)).astype(BF)


def sum_kernel(own_ref, a_ref, b_ref, c_ref, d_ref, out_ref, total_ref, sem):
    half = a_ref.shape[1]
    step = half // 2
    copies = []
    for i, (one, two) in enumerate(((c_ref, d_ref), (a_ref, b_ref))):
        base = half * (1 - i)
        for start in range(0, half, step):
            cols = slice(start, start + step)
            spot = slice(base + start, base + start + step)
            total = own_ref[:, spot].astype(F32) + one[:, cols].astype(F32)
            total_ref[:, spot] = (total + two[:, cols].astype(F32)).astype(BF)
            there = out_ref.at[:, pl.ds(base + start, step)]
            here = total_ref.at[:, pl.ds(base + start, step)]
            copies.append(pltpu.make_async_copy(here, there, sem.at[len(copies)]))
            copies[-1].start()
    for copy in copies:
        copy.wait()


def shape(*dims, dtype=BF):
    return jax.ShapeDtypeStruct(dims, dtype)


EARLY, LATE = (4, 0, 2, 1, 3), (5, 7, 6)


def attend(qs, kvs, before=None, met=None):
    count, early, merging = len(qs), before is None, met is not None
    chunks = EARLY if early else LATE
    keys = 256 * len(chunks)
    outs = (shape(144, 256),)
    if early:
        outs = (shape(HD, 256, dtype=F32), shape(8, 256, dtype=F32))
    operands = [*qs, *(kvs[i] for i in chunks)]
    operands += [] if early else [part for pair in before for part in pair]
    operands += [met] if merging else []
    return pl.pallas_call(
        functools.partial(attend_kernel, count, chunks, early, merging),
        out_shape=outs * count,
        in_specs=[VMEM] * len(operands),
        out_specs=(VMEM,) * (len(outs) * count),
        scratch_shapes=[
            pltpu.VMEM((HD, keys), BF),
            pltpu.VMEM((2, keys, 256), F32),
            pltpu.VMEM((2, keys, 256), BF),
            pltpu.VMEM((HD, 256 * count), F32),
        ],
        compiler_params=PARAMS,
        cost_estimate=pl.CostEstimate(
            flops=2 * 2 * 256 * count * keys * HD * 8,
            bytes_accessed=2**21,
            transcendentals=256 * count * keys,
        ),
    )(*operands)


def body(queries, keys, values, block_mask, out_weight):
    *pieces, marks = pl.pallas_call(
        prep_kernel,
        out_shape=tuple(shape(32, 768) for _ in range(4)) + (shape(16, HD),),
        in_specs=[pl.BlockSpec(memory_space=pl.ANY)] * 4,
        out_specs=(VMEM,) * 5,
        scratch_shapes=[
            pltpu.VMEM((3, 32, 1024), BF),
            pltpu.VMEM(block_mask.shape, jnp.int32),
            pltpu.SemaphoreType.DMA((4,)),
        ],
        compiler_params=PARAMS,
    )(*(pltpu.with_memory_space_constraint(t, pltpu.HBM) for t in (queries, keys, values, block_mask)))
    met = {m: swapped(pieces[m], "y", m) for m in (2, 3, 1)}
    mine, send = pl.pallas_call(
        pack_kernel,
        out_shape=(shape(144, 512), shape(144, 512)),
        in_specs=[VMEM] * 5,
        out_specs=(VMEM, VMEM),
        compiler_params=PARAMS,
    )(marks, pieces[0], met[1], met[2], met[3])
    got = moved(send, "c", 1)
    q, kv = pl.pallas_call(
        mid_kernel,
        out_shape=(shape(544, HD), shape(256, 256)),
        in_specs=[VMEM] * 2,
        out_specs=(VMEM, VMEM),
        compiler_params=PARAMS,
    )(mine, got)

    pair = swapped(kv, "zl", 1)
    near = {m: swapped(kv, "x", m) for m in (2, 1, 3)}
    far = {m: swapped(pair, "x", m) for m in (1, 3)}
    far[2] = swapped(near[2], "zl", 1)
    kvs = [kv, near[1], near[2], near[3], pair, far[1], far[2], far[3]]
    first = swapped_by_core(q, "zh", (1, 3))
    across = swapped_by_core(first[:272], "zh", (3, 1))
    second = moved(first[272:], "c", 1)

    raw = attend((q, first, second, across), kvs)
    raw = [raw[2 * i : 2 * i + 2] for i in (3, 1, 2, 0)]
    across, give = attend((across, first), kvs, raw[:2])
    across = swapped(across, "zh", 2)
    took = moved(give, "c", 1)
    (keep,) = attend((second,), kvs, raw[2:3])
    joined = pl.pallas_call(
        join_kernel,
        out_shape=shape(288, 256),
        in_specs=[VMEM] * 2,
        out_specs=VMEM,
        compiler_params=PARAMS,
    )(keep, took)
    side = swapped_by_core(joined, "zh", (3, 1))
    (own,) = attend((q,), kvs, raw[3:], across)
    send = pl.pallas_call(
        share_kernel,
        out_shape=shape(288, BLK),
        in_specs=[VMEM] * 2,
        out_specs=VMEM,
        compiler_params=PARAMS,
    )(own, side)
    got = moved(send, "c", 1)

    width = out_weight.shape[1]
    pieces = pl.pallas_call(
        project_kernel,
        out_shape=tuple(shape(32, width) for _ in range(4)),
        in_specs=[VMEM] * 4,
        out_specs=(VMEM,) * 4,
        scratch_shapes=[pltpu.VMEM((BLK, 2 * HD), BF)],
        compiler_params=PARAMS,
        cost_estimate=pl.CostEstimate(
            flops=2 * 128 * 256 * width, bytes_accessed=2**22, transcendentals=0
        ),
    )(own, side, got, out_weight)
    own, one, two, three = pieces
    half = width // 2
    b = swapped(two[:, half:], "y", 3)
    a = swapped(two[:, :half], "y", 1)
    right_three = swapped(three[:, half:], "y", 3)
    left_one = swapped(one[:, :half], "y", 1)
    by_one, by_three = pl.pallas_call(
        pass_kernel,
        out_shape=(shape(32, half), shape(32, half)),
        in_specs=[VMEM] * 4,
        out_specs=(VMEM, VMEM),
        compiler_params=PARAMS,
    )(one, three, a, b)
    left_three = swapped(by_three, "y", 3)
    right_one = swapped(by_one, "y", 1)
    return pl.pallas_call(
        sum_kernel,
        out_shape=shape(32, width),
        in_specs=[VMEM] * 5,
        out_specs=pl.BlockSpec(memory_space=pl.ANY),
        scratch_shapes=[pltpu.VMEM((32, width), BF), pltpu.SemaphoreType.DMA((4,))],
        compiler_params=PARAMS,
    )(own, left_one, left_three, right_one, right_three)


def solution(mesh):
    grid = Mesh(mesh.devices.reshape(SIZES), AXES)
    rows = P(AXES, None)
    in_specs = (rows, rows, rows, P("y", AXES[:4], None), P("y", None))
    return jax.shard_map(body, mesh=grid, in_specs=in_specs, out_specs=rows, check_vma=False)
```

```python
import functools
import math

import jax
import jax.numpy as jnp
from jax import lax
from jax.experimental import pallas as pl
from jax.experimental.pallas import tpu as pltpu
from jax.sharding import Mesh, PartitionSpec as P

HD = 128
BLK = 128
NX, NH, NL, NC, NY = 4, 4, 2, 2, 4
AXES = ("x", "zh", "zl", "c", "y")
SIZES = (NX, NH, NL, NC, NY)
BF = jnp.bfloat16
F32 = jnp.float32
SCALE2 = math.log2(math.e) / math.sqrt(HD)
NEG = -1e30
BIG = 1e30
VMEM = pl.BlockSpec(memory_space=pltpu.VMEM)
PARAMS = pltpu.CompilerParams(vmem_limit_bytes=40 * 2**20)


def moved(value, axis, by):
    size = SIZES[AXES.index(axis)]
    return lax.ppermute(value, axis, [(i, (i + by) % size) for i in range(size)])


def swapped(value, axis, mask):
    size = SIZES[AXES.index(axis)]
    return lax.ppermute(value, axis, [(i, i ^ mask) for i in range(size)])


def swapped_by_core(value, axis, masks):
    size = SIZES[AXES.index(axis)]
    pairs = [(i * NC + c, (i ^ masks[c]) * NC + c) for i in range(size) for c in range(NC)]
    return lax.ppermute(value, (axis, "c"), pairs)


def prep_kernel(q_ref, k_ref, v_ref, mask_ref, *refs):
    out_refs, marks_ref, held_ref, seen_ref, sem = refs[:4], *refs[4:]
    y, c = lax.axis_index("y"), lax.axis_index("c")
    copies = [
        pltpu.make_async_copy(ref, held_ref.at[i], sem.at[i])
        for i, ref in enumerate((q_ref, k_ref, v_ref))
    ]
    copies.append(pltpu.make_async_copy(mask_ref, seen_ref, sem.at[3]))
    for copy in copies:
        copy.start()
    copies.pop().wait()
    seen = seen_ref[:, 0, :].astype(F32)
    seen = jnp.concatenate([seen, jnp.zeros_like(seen)], axis=1)
    low = lax.broadcasted_iota(jnp.int32, (16, HD), 0) < 8
    marks_ref[...] = jnp.where(low, seen[0:1], seen[1:2]).astype(BF)
    for i, copy in enumerate(copies):
        copy.wait()
        for mask, out_ref in enumerate(out_refs):
            for mate in range(2):
                head = (y ^ mask) * 2 + (c ^ mate)
                cols = pl.ds(pl.multiple_of(head * HD, HD), HD)
                slot = mate if i == 0 else 1 + 2 * mate + i
                out_ref[:, slot * HD : (slot + 1) * HD] = held_ref[i, :, cols]


def pack_kernel(marks_ref, *refs):
    piece_refs, (mine_ref, send_ref) = refs[:4], refs[4:]
    for mask, ref in zip((0, 2, 3, 1), piece_refs):
        rows = slice(mask * 32, (mask + 1) * 32)
        mine_ref[rows, :] = ref[:, : 4 * HD]
        send_ref[rows, :HD] = ref[:, HD : 2 * HD]
        send_ref[rows, HD : 2 * HD] = ref[:, :HD]
        send_ref[rows, 2 * HD :] = ref[:, 4 * HD :]
    for ref in (mine_ref, send_ref):
        for slot in range(4):
            ref[BLK:, slot * HD : (slot + 1) * HD] = marks_ref[...]


def mid_kernel(mine_ref, got_ref, q_ref, kv_ref):
    for core in range(NC):

        @pl.when(lax.axis_index("c") == core)
        def _():
            for part, ref in enumerate((mine_ref, got_ref)):
                row = (core ^ part) * BLK
                q_ref[row : row + BLK, :] = ref[:BLK, :HD]
                q_ref[272 + row : 272 + row + BLK, :] = ref[:BLK, HD : 2 * HD]
                kv_ref[row : row + BLK, :] = ref[:BLK, 2 * HD :]
            marks = [ref[BLK:, :HD].astype(F32) for ref in (mine_ref, got_ref)]
            low = lax.broadcasted_iota(jnp.int32, (16, HD), 0) < 8
            for mate in range(2):
                row = (core ^ mate) * 8
                both = [marks[core][row : row + 1], marks[1 - core][row : row + 1]]
                q_ref[256 + 272 * mate : 272 + 272 * mate, :] = jnp.where(low, *both).astype(BF)


def attend_kernel(count, chunks, early, merging, *refs):
    refs = list(refs)
    q_refs = [refs.pop(0) for _ in range(count)]
    kv_refs = [refs.pop(0) for _ in chunks]
    before = [] if early else [(refs.pop(0), refs.pop(0)) for _ in range(count)]
    met_ref = refs.pop(0) if merging else None
    out_refs = [refs.pop(0) for _ in range(count * (1 + early))]
    vt_ref, s_ref, p_ref, open_ref = refs
    x, zh, zl = (lax.axis_index(a) for a in ("x", "zh", "zl"))
    for i, ref in enumerate(kv_refs):
        vt_ref[:, i * 256 : (i + 1) * 256] = ref[:, HD:].T
    masks = [ref[256:272, :] for ref in q_refs]
    masks = jnp.concatenate(masks, axis=0) if count > 1 else masks[0]
    row = lax.broadcasted_iota(jnp.int32, (16 * count, 256 * count), 0)
    block = lax.broadcasted_iota(jnp.int32, (16 * count, 256 * count), 1) // BLK
    pick = jnp.where(row == block * 8, 1.0, 0.0).astype(BF)
    open_ref[...] = lax.dot_general(
        masks, pick, (((0,), (0,)), ((), ())), preferred_element_type=F32
    )

    def score(j):
        q = q_refs[j][:256, :]
        opens = []
        top = jnp.full((1, 256), NEG, F32)
        for i, chunk in enumerate(chunks):
            source = (x ^ (chunk % 4)) * 16 + zh * 4 + (zl ^ (chunk // 4)) * 2
            s = lax.dot_general(
                kv_refs[i][:, :HD], q, (((1,), (1,)), ((), ())), preferred_element_type=F32
            )
            s_ref[j % 2, i * 256 : (i + 1) * 256, :] = s
            for part in range(2):
                is_open = open_ref[pl.ds(source + part, 1), j * 256 : (j + 1) * 256] > 0.5
                opens.append(is_open)
                here = jnp.max(s[part * BLK : (part + 1) * BLK], axis=0, keepdims=True)
                top = jnp.maximum(top, jnp.where(is_open, here, NEG))
        return opens, top * SCALE2

    following = score(0)
    for j in range(count):
        opens, top = following
        if j < count - 1:
            following = score(j + 1)
        sums = jnp.zeros((8, 256), F32)
        for b in range(2 * len(chunks)):
            less = jnp.where(opens[b], top, BIG)
            rows = slice(b * BLK, (b + 1) * BLK)
            w = jnp.exp2(s_ref[j % 2, rows, :] * SCALE2 - less)
            sums += jnp.sum(w.reshape(16, 8, 256), axis=0)
            p_ref[j % 2, rows, :] = w.astype(BF)
        total = jnp.sum(sums, axis=0, keepdims=True)
        acc = jnp.dot(vt_ref[...], p_ref[j % 2], preferred_element_type=F32)
        if early:
            row = lax.broadcasted_iota(jnp.int32, (8, 256), 0)
            out_refs[2 * j][...] = acc
            out_refs[2 * j + 1][...] = jnp.where(row == 0, top, total)
            continue
        acc_ref, stat_ref = before[j]
        top0, total0 = stat_ref[0:1, :], stat_ref[1:2, :]
        both = jnp.maximum(top, top0)
        keep, keep0 = jnp.exp2(top - both), jnp.exp2(top0 - both)
        acc = acc * keep + acc_ref[...] * keep0
        top, total = both, total * keep + total0 * keep0
        some = total > 0.0
        safe = jnp.where(some, total, 1.0)
        acc = acc / safe
        lse = jnp.where(some, top + jnp.log2(safe), NEG)
        if merging:
            tail = met_ref[HD:, :].astype(F32)
            met = tail[0:1] + tail[1:2] + tail[2:3]
            top = jnp.maximum(lse, met)
            mine, theirs = jnp.exp2(lse - top), jnp.exp2(met - top)
            total = mine + theirs
            acc = acc * (mine / total) + met_ref[:HD, :].astype(F32) * (theirs / total)
            lse = top + jnp.log2(total)
        out_refs[j][:HD, :] = acc.astype(BF)
        out_refs[j][HD:, :] = packed_tail(lse)


def packed_tail(lse):
    hi = lse.astype(BF).astype(F32)
    mid = (lse - hi).astype(BF).astype(F32)
    row = lax.broadcasted_iota(jnp.int32, (16, lse.shape[1]), 0)
    return jnp.where(row == 0, hi, jnp.where(row == 1, mid, lse - hi - mid)).astype(BF)


def merged(parts):
    lses = []
    for part in parts:
        tail = part[HD:, :].astype(F32)
        lses.append(tail[0:1] + tail[1:2] + tail[2:3])
    top = functools.reduce(jnp.maximum, lses)
    ws = [jnp.exp2(lse - top) for lse in lses]
    total = sum(ws)
    inv = 1.0 / total
    acc = sum(part[:HD, :].astype(F32) * (w * inv) for part, w in zip(parts, ws))
    return acc.astype(BF), top + jnp.log2(total)


def join_kernel(a_ref, b_ref, out_ref):
    out_ref[:144, :] = a_ref[...]
    out_ref[144:, :] = b_ref[...]


def share_kernel(own_ref, side_ref, send_ref):
    for core in range(NC):

        @pl.when(lax.axis_index("c") == core)
        def _():
            cols = slice((1 - core) * BLK, (2 - core) * BLK)
            acc, lse = merged([own_ref[:, cols], side_ref[:144, cols]])
            send_ref[:HD, :] = acc
            send_ref[HD:144, :] = packed_tail(lse)
            send_ref[144:, :] = side_ref[144:, cols]


def project_kernel(own_ref, side_ref, got_ref, w_ref, *refs):
    out_refs, lhs_ref = refs[:4], refs[4]
    for core in range(NC):

        @pl.when(lax.axis_index("c") == core)
        def _():
            cols = slice(core * BLK, (core + 1) * BLK)
            mine = [own_ref[:, cols], side_ref[:144, cols], got_ref[144:]]
            mate = [side_ref[144:, cols], got_ref[:144]]
            lhs_ref[:, core * HD : (core + 1) * HD] = merged(mine)[0].T
            lhs_ref[:, (1 - core) * HD : (2 - core) * HD] = merged(mate)[0].T

    lhs = lhs_ref[...]
    for start in range(0, w_ref.shape[1], 512):
        cols = slice(start, start + 512)
        out = jnp.dot(lhs, w_ref[:, cols], preferred_element_type=F32).astype(BF)
        for p in range(NY):
            out_refs[p][:, cols] = out[p * 32 : (p + 1) * 32]


def pass_kernel(one_ref, three_ref, a_ref, b_ref, by_one_ref, by_three_ref):
    half = a_ref.shape[1]
    by_one_ref[...] = (one_ref[:, half:].astype(F32) + b_ref[...].astype(F32)).astype(BF)
    by_three_ref[...] = (three_ref[:, :half].astype(F32) + a_ref[...].astype(F32)).astype(BF)


def sum_kernel(own_ref, a_ref, b_ref, c_ref, d_ref, out_ref, total_ref, sem):
    half = a_ref.shape[1]
    step = half // 2
    copies = []
    for i, (one, two) in enumerate(((c_ref, d_ref), (a_ref, b_ref))):
        base = half * (1 - i)
        for start in range(0, half, step):
            cols = slice(start, start + step)
            spot = slice(base + start, base + start + step)
            total = own_ref[:, spot].astype(F32) + one[:, cols].astype(F32)
            total_ref[:, spot] = (total + two[:, cols].astype(F32)).astype(BF)
            there = out_ref.at[:, pl.ds(base + start, step)]
            here = total_ref.at[:, pl.ds(base + start, step)]
            copies.append(pltpu.make_async_copy(here, there, sem.at[len(copies)]))
            copies[-1].start()
    for copy in copies:
        copy.wait()


def shape(*dims, dtype=BF):
    return jax.ShapeDtypeStruct(dims, dtype)


EARLY, LATE = (4, 0, 2, 1, 3), (5, 7, 6)


def attend(qs, kvs, before=None, met=None):
    count, early, merging = len(qs), before is None, met is not None
    chunks = EARLY if early else LATE
    keys = 256 * len(chunks)
    outs = (shape(144, 256),)
    if early:
        outs = (shape(HD, 256, dtype=F32), shape(8, 256, dtype=F32))
    operands = [*qs, *(kvs[i] for i in chunks)]
    operands += [] if early else [part for pair in before for part in pair]
    operands += [met] if merging else []
    return pl.pallas_call(
        functools.partial(attend_kernel, count, chunks, early, merging),
        out_shape=outs * count,
        in_specs=[VMEM] * len(operands),
        out_specs=(VMEM,) * (len(outs) * count),
        scratch_shapes=[
            pltpu.VMEM((HD, keys), BF),
            pltpu.VMEM((2, keys, 256), F32),
            pltpu.VMEM((2, keys, 256), BF),
            pltpu.VMEM((HD, 256 * count), F32),
        ],
        compiler_params=PARAMS,
        cost_estimate=pl.CostEstimate(
            flops=2 * 2 * 256 * count * keys * HD * 8,
            bytes_accessed=2**21,
            transcendentals=256 * count * keys,
        ),
    )(*operands)


def body(queries, keys, values, block_mask, out_weight):
    *pieces, marks = pl.pallas_call(
        prep_kernel,
        out_shape=tuple(shape(32, 768) for _ in range(4)) + (shape(16, HD),),
        in_specs=[pl.BlockSpec(memory_space=pl.ANY)] * 4,
        out_specs=(VMEM,) * 5,
        scratch_shapes=[
            pltpu.VMEM((3, 32, 1024), BF),
            pltpu.VMEM(block_mask.shape, jnp.int32),
            pltpu.SemaphoreType.DMA((4,)),
        ],
        compiler_params=PARAMS,
    )(*(pltpu.with_memory_space_constraint(t, pltpu.HBM) for t in (queries, keys, values, block_mask)))
    met = {m: swapped(pieces[m], "y", m) for m in (2, 3, 1)}
    mine, send = pl.pallas_call(
        pack_kernel,
        out_shape=(shape(144, 512), shape(144, 512)),
        in_specs=[VMEM] * 5,
        out_specs=(VMEM, VMEM),
        compiler_params=PARAMS,
    )(marks, pieces[0], met[2], met[3], met[1])
    got = moved(send, "c", 1)
    q, kv = pl.pallas_call(
        mid_kernel,
        out_shape=(shape(544, HD), shape(256, 256)),
        in_specs=[VMEM] * 2,
        out_specs=(VMEM, VMEM),
        compiler_params=PARAMS,
    )(mine, got)

    pair = swapped(kv, "zl", 1)
    near = {m: swapped(kv, "x", m) for m in (2, 1, 3)}
    far = {m: swapped(pair, "x", m) for m in (1, 3)}
    far[2] = swapped(near[2], "zl", 1)
    kvs = [kv, near[1], near[2], near[3], pair, far[1], far[2], far[3]]
    first = swapped_by_core(q, "zh", (1, 3))
    across = swapped_by_core(first[:272], "zh", (3, 1))
    second = moved(first[272:], "c", 1)

    raw = attend((across, second, q, first), kvs)
    raw = [raw[2 * i : 2 * i + 2] for i in (0, 3, 1, 2)]
    across, give = attend((across, first), kvs, raw[:2])
    across = swapped(across, "zh", 2)
    took = moved(give, "c", 1)
    (keep,) = attend((second,), kvs, raw[2:3])
    joined = pl.pallas_call(
        join_kernel,
        out_shape=shape(288, 256),
        in_specs=[VMEM] * 2,
        out_specs=VMEM,
        compiler_params=PARAMS,
    )(keep, took)
    side = swapped_by_core(joined, "zh", (3, 1))
    (own,) = attend((q,), kvs, raw[3:], across)
    send = pl.pallas_call(
        share_kernel,
        out_shape=shape(288, BLK),
        in_specs=[VMEM] * 2,
        out_specs=VMEM,
        compiler_params=PARAMS,
    )(own, side)
    got = moved(send, "c", 1)

    width = out_weight.shape[1]
    pieces = pl.pallas_call(
        project_kernel,
        out_shape=tuple(shape(32, width) for _ in range(4)),
        in_specs=[VMEM] * 4,
        out_specs=(VMEM,) * 4,
        scratch_shapes=[pltpu.VMEM((BLK, 2 * HD), BF)],
        compiler_params=PARAMS,
        cost_estimate=pl.CostEstimate(
            flops=2 * 128 * 256 * width, bytes_accessed=2**22, transcendentals=0
        ),
    )(own, side, got, out_weight)
    own, one, two, three = pieces
    half = width // 2
    b = swapped(two[:, half:], "y", 3)
    a = swapped(two[:, :half], "y", 1)
    right_three = swapped(three[:, half:], "y", 3)
    left_one = swapped(one[:, :half], "y", 1)
    by_one, by_three = pl.pallas_call(
        pass_kernel,
        out_shape=(shape(32, half), shape(32, half)),
        in_specs=[VMEM] * 4,
        out_specs=(VMEM, VMEM),
        compiler_params=PARAMS,
    )(one, three, a, b)
    left_three = swapped(by_three, "y", 3)
    right_one = swapped(by_one, "y", 1)
    return pl.pallas_call(
        sum_kernel,
        out_shape=shape(32, width),
        in_specs=[VMEM] * 5,
        out_specs=pl.BlockSpec(memory_space=pl.ANY),
        scratch_shapes=[pltpu.VMEM((32, width), BF), pltpu.SemaphoreType.DMA((4,))],
        compiler_params=PARAMS,
    )(own, left_one, left_three, right_one, right_three)


def solution(mesh):
    grid = Mesh(mesh.devices.reshape(SIZES), AXES)
    rows = P(AXES, None)
    in_specs = (rows, rows, rows, P("y", AXES[:4], None), P("y", None))
    return jax.shard_map(body, mesh=grid, in_specs=in_specs, out_specs=rows, check_vma=False)
```

```python
import functools
import math

import jax
import jax.numpy as jnp
from jax import lax
from jax.experimental import pallas as pl
from jax.experimental.pallas import tpu as pltpu
from jax.sharding import Mesh, PartitionSpec as P

HD = 128
BLK = 128
NX, NH, NL, NC, NY = 4, 4, 2, 2, 4
AXES = ("x", "zh", "zl", "c", "y")
SIZES = (NX, NH, NL, NC, NY)
BF = jnp.bfloat16
F32 = jnp.float32
SCALE2 = math.log2(math.e) / math.sqrt(HD)
NEG = -1e30
BIG = 1e30
VMEM = pl.BlockSpec(memory_space=pltpu.VMEM)
PARAMS = pltpu.CompilerParams(vmem_limit_bytes=40 * 2**20)


def moved(value, axis, by):
    size = SIZES[AXES.index(axis)]
    return lax.ppermute(value, axis, [(i, (i + by) % size) for i in range(size)])


def swapped(value, axis, mask):
    size = SIZES[AXES.index(axis)]
    return lax.ppermute(value, axis, [(i, i ^ mask) for i in range(size)])


def swapped_by_core(value, axis, masks):
    size = SIZES[AXES.index(axis)]
    pairs = [(i * NC + c, (i ^ masks[c]) * NC + c) for i in range(size) for c in range(NC)]
    return lax.ppermute(value, (axis, "c"), pairs)


def prep_kernel(q_ref, k_ref, v_ref, mask_ref, *refs):
    out_refs, marks_ref, held_ref, seen_ref, sem = refs[:4], *refs[4:]
    y, c = lax.axis_index("y"), lax.axis_index("c")
    copies = [
        pltpu.make_async_copy(ref, held_ref.at[i], sem.at[i])
        for i, ref in enumerate((q_ref, k_ref, v_ref))
    ]
    copies.append(pltpu.make_async_copy(mask_ref, seen_ref, sem.at[3]))
    for copy in copies:
        copy.start()
    copies.pop().wait()
    seen = seen_ref[:, 0, :].astype(F32)
    seen = jnp.concatenate([seen, jnp.zeros_like(seen)], axis=1)
    low = lax.broadcasted_iota(jnp.int32, (16, HD), 0) < 8
    marks_ref[...] = jnp.where(low, seen[0:1], seen[1:2]).astype(BF)
    for i, copy in enumerate(copies):
        copy.wait()
        for mask, out_ref in enumerate(out_refs):
            for mate in range(2):
                head = (y ^ mask) * 2 + (c ^ mate)
                cols = pl.ds(pl.multiple_of(head * HD, HD), HD)
                slot = mate if i == 0 else 1 + 2 * mate + i
                out_ref[:, slot * HD : (slot + 1) * HD] = held_ref[i, :, cols]


def pack_kernel(marks_ref, *refs):
    piece_refs, (mine_ref, send_ref) = refs[:4], refs[4:]
    for mask, ref in zip((0, 2, 3, 1), piece_refs):
        rows = slice(mask * 32, (mask + 1) * 32)
        mine_ref[rows, :] = ref[:, : 4 * HD]
        send_ref[rows, :HD] = ref[:, HD : 2 * HD]
        send_ref[rows, HD : 2 * HD] = ref[:, :HD]
        send_ref[rows, 2 * HD :] = ref[:, 4 * HD :]
    for ref in (mine_ref, send_ref):
        for slot in range(4):
            ref[BLK:, slot * HD : (slot + 1) * HD] = marks_ref[...]


def mid_kernel(mine_ref, got_ref, q_ref, kv_ref):
    for core in range(NC):

        @pl.when(lax.axis_index("c") == core)
        def _():
            for part, ref in enumerate((mine_ref, got_ref)):
                row = (core ^ part) * BLK
                q_ref[row : row + BLK, :] = ref[:BLK, :HD]
                q_ref[272 + row : 272 + row + BLK, :] = ref[:BLK, HD : 2 * HD]
                kv_ref[row : row + BLK, :] = ref[:BLK, 2 * HD :]
            marks = [ref[BLK:, :HD].astype(F32) for ref in (mine_ref, got_ref)]
            low = lax.broadcasted_iota(jnp.int32, (16, HD), 0) < 8
            for mate in range(2):
                row = (core ^ mate) * 8
                both = [marks[core][row : row + 1], marks[1 - core][row : row + 1]]
                q_ref[256 + 272 * mate : 272 + 272 * mate, :] = jnp.where(low, *both).astype(BF)


def attend_kernel(count, chunks, early, merging, *refs):
    refs = list(refs)
    q_refs = [refs.pop(0) for _ in range(count)]
    kv_refs = [refs.pop(0) for _ in chunks]
    before = [] if early else [(refs.pop(0), refs.pop(0)) for _ in range(count)]
    met_ref = refs.pop(0) if merging else None
    out_refs = [refs.pop(0) for _ in range(count * (1 + early))]
    vt_ref, s_ref, p_ref, open_ref = refs
    x, zh, zl = (lax.axis_index(a) for a in ("x", "zh", "zl"))
    for i, ref in enumerate(kv_refs):
        vt_ref[:, i * 256 : (i + 1) * 256] = ref[:, HD:].T
    masks = [ref[256:272, :] for ref in q_refs]
    masks = jnp.concatenate(masks, axis=0) if count > 1 else masks[0]
    row = lax.broadcasted_iota(jnp.int32, (16 * count, 256 * count), 0)
    block = lax.broadcasted_iota(jnp.int32, (16 * count, 256 * count), 1) // BLK
    pick = jnp.where(row == block * 8, 1.0, 0.0).astype(BF)
    open_ref[...] = lax.dot_general(
        masks, pick, (((0,), (0,)), ((), ())), preferred_element_type=F32
    )

    def score(j):
        q = q_refs[j][:256, :]
        opens = []
        top = jnp.full((1, 256), NEG, F32)
        for i, chunk in enumerate(chunks):
            source = (x ^ (chunk % 4)) * 16 + zh * 4 + (zl ^ (chunk // 4)) * 2
            s = lax.dot_general(
                kv_refs[i][:, :HD], q, (((1,), (1,)), ((), ())), preferred_element_type=F32
            )
            s_ref[j % 2, i * 256 : (i + 1) * 256, :] = s
            for part in range(2):
                is_open = open_ref[pl.ds(source + part, 1), j * 256 : (j + 1) * 256] > 0.5
                opens.append(is_open)
                here = jnp.max(s[part * BLK : (part + 1) * BLK], axis=0, keepdims=True)
                top = jnp.maximum(top, jnp.where(is_open, here, NEG))
        return opens, top * SCALE2

    following = score(0)
    for j in range(count):
        opens, top = following
        if j < count - 1:
            following = score(j + 1)
        sums = jnp.zeros((8, 256), F32)
        for b in range(2 * len(chunks)):
            less = jnp.where(opens[b], top, BIG)
            rows = slice(b * BLK, (b + 1) * BLK)
            w = jnp.exp2(s_ref[j % 2, rows, :] * SCALE2 - less)
            sums += jnp.sum(w.reshape(16, 8, 256), axis=0)
            p_ref[j % 2, rows, :] = w.astype(BF)
        total = jnp.sum(sums, axis=0, keepdims=True)
        acc = jnp.dot(vt_ref[...], p_ref[j % 2], preferred_element_type=F32)
        if early:
            row = lax.broadcasted_iota(jnp.int32, (8, 256), 0)
            out_refs[2 * j][...] = acc
            out_refs[2 * j + 1][...] = jnp.where(row == 0, top, total)
            continue
        acc_ref, stat_ref = before[j]
        top0, total0 = stat_ref[0:1, :], stat_ref[1:2, :]
        both = jnp.maximum(top, top0)
        keep, keep0 = jnp.exp2(top - both), jnp.exp2(top0 - both)
        acc = acc * keep + acc_ref[...] * keep0
        top, total = both, total * keep + total0 * keep0
        some = total > 0.0
        safe = jnp.where(some, total, 1.0)
        acc = acc / safe
        lse = jnp.where(some, top + jnp.log2(safe), NEG)
        if merging:
            tail = met_ref[HD:, :].astype(F32)
            met = tail[0:1] + tail[1:2] + tail[2:3]
            top = jnp.maximum(lse, met)
            mine, theirs = jnp.exp2(lse - top), jnp.exp2(met - top)
            total = mine + theirs
            acc = acc * (mine / total) + met_ref[:HD, :].astype(F32) * (theirs / total)
            lse = top + jnp.log2(total)
        out_refs[j][:HD, :] = acc.astype(BF)
        out_refs[j][HD:, :] = packed_tail(lse)


def packed_tail(lse):
    hi = lse.astype(BF).astype(F32)
    mid = (lse - hi).astype(BF).astype(F32)
    row = lax.broadcasted_iota(jnp.int32, (16, lse.shape[1]), 0)
    return jnp.where(row == 0, hi, jnp.where(row == 1, mid, lse - hi - mid)).astype(BF)


def merged(parts):
    lses = []
    for part in parts:
        tail = part[HD:, :].astype(F32)
        lses.append(tail[0:1] + tail[1:2] + tail[2:3])
    top = functools.reduce(jnp.maximum, lses)
    ws = [jnp.exp2(lse - top) for lse in lses]
    total = sum(ws)
    inv = 1.0 / total
    acc = sum(part[:HD, :].astype(F32) * (w * inv) for part, w in zip(parts, ws))
    return acc.astype(BF), top + jnp.log2(total)


def join_kernel(a_ref, b_ref, out_ref):
    out_ref[:144, :] = a_ref[...]
    out_ref[144:, :] = b_ref[...]


def share_kernel(own_ref, side_ref, send_ref):
    for core in range(NC):

        @pl.when(lax.axis_index("c") == core)
        def _():
            cols = slice((1 - core) * BLK, (2 - core) * BLK)
            acc, lse = merged([own_ref[:, cols], side_ref[:144, cols]])
            send_ref[:HD, :] = acc
            send_ref[HD:144, :] = packed_tail(lse)
            send_ref[144:, :] = side_ref[144:, cols]


def project_kernel(own_ref, side_ref, got_ref, w_ref, *refs):
    out_refs, lhs_ref = refs[:4], refs[4]
    for core in range(NC):

        @pl.when(lax.axis_index("c") == core)
        def _():
            cols = slice(core * BLK, (core + 1) * BLK)
            mine = [own_ref[:, cols], side_ref[:144, cols], got_ref[144:]]
            mate = [side_ref[144:, cols], got_ref[:144]]
            lhs_ref[:, core * HD : (core + 1) * HD] = merged(mine)[0].T
            lhs_ref[:, (1 - core) * HD : (2 - core) * HD] = merged(mate)[0].T

    lhs = lhs_ref[...]
    for start in range(0, w_ref.shape[1], 512):
        cols = slice(start, start + 512)
        out = jnp.dot(lhs, w_ref[:, cols], preferred_element_type=F32).astype(BF)
        for p in range(NY):
            out_refs[p][:, cols] = out[p * 32 : (p + 1) * 32]


def pass_kernel(one_ref, three_ref, a_ref, b_ref, by_one_ref, by_three_ref):
    half = a_ref.shape[1]
    by_one_ref[...] = (one_ref[:, half:].astype(F32) + b_ref[...].astype(F32)).astype(BF)
    by_three_ref[...] = (three_ref[:, :half].astype(F32) + a_ref[...].astype(F32)).astype(BF)


def sum_kernel(base, own_ref, a_ref, b_ref, *refs):
    out_ref, total_ref, sem = refs[-3:]
    half = a_ref.shape[1]
    step = half // 2
    copies = []
    for i in range(2):
        cols = slice(i * step, (i + 1) * step)
        total = own_ref[:, base + i * step : base + (i + 1) * step].astype(F32)
        total += a_ref[:, cols].astype(F32) + b_ref[:, cols].astype(F32)
        total_ref[:, cols] = total.astype(BF)
        there = out_ref.at[:, pl.ds(base + i * step, step)]
        copies.append(pltpu.make_async_copy(total_ref.at[:, pl.ds(i * step, step)], there, sem.at[i]))
        copies[-1].start()
    for copy in copies:
        copy.wait()


def shape(*dims, dtype=BF):
    return jax.ShapeDtypeStruct(dims, dtype)


EARLY, LATE = (4, 0, 2, 1, 3), (5, 7, 6)


def attend(qs, kvs, before=None, met=None):
    count, early, merging = len(qs), before is None, met is not None
    chunks = EARLY if early else LATE
    keys = 256 * len(chunks)
    outs = (shape(144, 256),)
    if early:
        outs = (shape(HD, 256, dtype=F32), shape(8, 256, dtype=F32))
    operands = [*qs, *(kvs[i] for i in chunks)]
    operands += [] if early else [part for pair in before for part in pair]
    operands += [met] if merging else []
    return pl.pallas_call(
        functools.partial(attend_kernel, count, chunks, early, merging),
        out_shape=outs * count,
        in_specs=[VMEM] * len(operands),
        out_specs=(VMEM,) * (len(outs) * count),
        scratch_shapes=[
            pltpu.VMEM((HD, keys), BF),
            pltpu.VMEM((2, keys, 256), F32),
            pltpu.VMEM((2, keys, 256), BF),
            pltpu.VMEM((HD, 256 * count), F32),
        ],
        compiler_params=PARAMS,
        cost_estimate=pl.CostEstimate(
            flops=2 * 2 * 256 * count * keys * HD * 8,
            bytes_accessed=2**21,
            transcendentals=256 * count * keys,
        ),
    )(*operands)


def body(queries, keys, values, block_mask, out_weight):
    *pieces, marks = pl.pallas_call(
        prep_kernel,
        out_shape=tuple(shape(32, 768) for _ in range(4)) + (shape(16, HD),),
        in_specs=[pl.BlockSpec(memory_space=pl.ANY)] * 4,
        out_specs=(VMEM,) * 5,
        scratch_shapes=[
            pltpu.VMEM((3, 32, 1024), BF),
            pltpu.VMEM(block_mask.shape, jnp.int32),
            pltpu.SemaphoreType.DMA((4,)),
        ],
        compiler_params=PARAMS,
    )(*(pltpu.with_memory_space_constraint(t, pltpu.HBM) for t in (queries, keys, values, block_mask)))
    met = {m: swapped(pieces[m], "y", m) for m in (2, 3, 1)}
    mine, send = pl.pallas_call(
        pack_kernel,
        out_shape=(shape(144, 512), shape(144, 512)),
        in_specs=[VMEM] * 5,
        out_specs=(VMEM, VMEM),
        compiler_params=PARAMS,
    )(marks, pieces[0], met[2], met[3], met[1])
    got = moved(send, "c", 1)
    q, kv = pl.pallas_call(
        mid_kernel,
        out_shape=(shape(544, HD), shape(256, 256)),
        in_specs=[VMEM] * 2,
        out_specs=(VMEM, VMEM),
        compiler_params=PARAMS,
    )(mine, got)

    pair = swapped(kv, "zl", 1)
    near = {m: swapped(kv, "x", m) for m in (2, 1, 3)}
    far = {m: swapped(pair, "x", m) for m in (1, 3)}
    far[2] = swapped(near[2], "zl", 1)
    kvs = [kv, near[1], near[2], near[3], pair, far[1], far[2], far[3]]
    first = swapped_by_core(q, "zh", (1, 3))
    across = swapped_by_core(first[:272], "zh", (3, 1))
    second = moved(first[272:], "c", 1)

    raw = attend((across, second, q, first), kvs)
    raw = [raw[2 * i : 2 * i + 2] for i in (0, 3, 1, 2)]
    across, give = attend((across, first), kvs, raw[:2])
    across = swapped(across, "zh", 2)
    took = moved(give, "c", 1)
    (keep,) = attend((second,), kvs, raw[2:3])
    joined = pl.pallas_call(
        join_kernel,
        out_shape=shape(288, 256),
        in_specs=[VMEM] * 2,
        out_specs=VMEM,
        compiler_params=PARAMS,
    )(keep, took)
    side = swapped_by_core(joined, "zh", (3, 1))
    (own,) = attend((q,), kvs, raw[3:], across)
    send = pl.pallas_call(
        share_kernel,
        out_shape=shape(288, BLK),
        in_specs=[VMEM] * 2,
        out_specs=VMEM,
        compiler_params=PARAMS,
    )(own, side)
    got = moved(send, "c", 1)

    width = out_weight.shape[1]
    pieces = pl.pallas_call(
        project_kernel,
        out_shape=tuple(shape(32, width) for _ in range(4)),
        in_specs=[VMEM] * 4,
        out_specs=(VMEM,) * 4,
        scratch_shapes=[pltpu.VMEM((BLK, 2 * HD), BF)],
        compiler_params=PARAMS,
        cost_estimate=pl.CostEstimate(
            flops=2 * 128 * 256 * width, bytes_accessed=2**22, transcendentals=0
        ),
    )(own, side, got, out_weight)
    own, one, two, three = pieces
    half = width // 2
    b = swapped(two[:, half:], "y", 3)
    a = swapped(two[:, :half], "y", 1)
    right_three = swapped(three[:, half:], "y", 3)
    left_one = swapped(one[:, :half], "y", 1)
    by_one, by_three = pl.pallas_call(
        pass_kernel,
        out_shape=(shape(32, half), shape(32, half)),
        in_specs=[VMEM] * 4,
        out_specs=(VMEM, VMEM),
        compiler_params=PARAMS,
    )(one, three, a, b)
    left_three = swapped(by_three, "y", 3)
    right_one = swapped(by_one, "y", 1)
    out = ()
    for base, pair in ((half, (right_one, right_three)), (0, (left_one, left_three))):
        out = pl.pallas_call(
            functools.partial(sum_kernel, base),
            out_shape=(shape(32, width),),
            in_specs=[VMEM] * 3 + [pl.BlockSpec(memory_space=pl.ANY)] * len(out),
            out_specs=(pl.BlockSpec(memory_space=pl.ANY),),
            scratch_shapes=[pltpu.VMEM((32, half), BF), pltpu.SemaphoreType.DMA((2,))],
            input_output_aliases={3: 0} if out else {},
            compiler_params=PARAMS,
        )(own, *pair, *out)
    return out[0]


def solution(mesh):
    grid = Mesh(mesh.devices.reshape(SIZES), AXES)
    rows = P(AXES, None)
    in_specs = (rows, rows, rows, P("y", AXES[:4], None), P("y", None))
    return jax.shard_map(body, mesh=grid, in_specs=in_specs, out_specs=rows, check_vma=False)
```
